256 devices in a mesh: ctx: 16 (over y, z_lo), fsdp: 16 (over x, z_hi, core).
Axes of the slice: x: 4, y: 4, z: 8 (z_hi: 2, z_lo: 4; z = z_hi * 4 + z_lo), core: 2. Of those that a mesh axis runs over, the one named last changes fastest.
Arguments:
- features: bfloat16 [16, 2048, 12288], P('fsdp', 'ctx'), may hold values from -6 to 6
- short_weight: bfloat16 [7, 12288], P(None, 'fsdp'), may hold values from -2 to 2
- long_filter: bfloat16 [512, 256], replicated, may hold values from -1.1 to 1.1
- out_weight: bfloat16 [4096, 4096], P(None, 'fsdp'), may hold values from -0.09375 to 0.09375
Outputs:
- mixer_out: bfloat16 [16, 2048, 4096], P('fsdp', 'ctx')
The draws below stay inside these ranges and needn't reach their ends.
All inputs are finite; a program needn't handle non-finite values.
Results may differ from the reference program's by a relative error of at most 0.0057.
Values may be sent and summed in bfloat16 or wider, within the bound.
A program may use at most 192 MiB of HBM per device.

```python
import jax
import jax.numpy as jnp
from jax import lax

TOK_DEV = 128
CHANNELS = 4096
FILTERS = 256
OUT_WIDTH = 4096
TAPS = 7
FILTER_LENGTH = 512
SEQ = 2048
BATCH = 16


def draw_long_filter(key, part):
    key = jax.random.fold_in(key, 11)
    complete_keys = jax.random.split(key, 5)
    delayed_rows = jnp.arange(FILTER_LENGTH, dtype=jnp.float32)[:, None]
    keeping = jax.random.randint(complete_keys[0], (1, FILTERS), 0, 10) < 5
    fast_rate = jax.random.uniform(complete_keys[1], (1, FILTERS), jnp.float32, 2.5, 4.3) / TOK_DEV
    slow_rate = jnp.exp(jax.random.uniform(complete_keys[2], (1, FILTERS), jnp.float32, jnp.log(0.05), 0.0)) / FILTER_LENGTH
    decay_rate = jnp.where(keeping, slow_rate, fast_rate)
    pulse_trains = jax.random.randint(complete_keys[3], (2,), 1, FILTER_LENGTH).astype(jnp.float32)
    decay_profile = jnp.exp(-decay_rate * delayed_rows)
    decay_profile = decay_profile * jnp.where(delayed_rows >= pulse_trains[0], 0.7, 1.0) * jnp.where(delayed_rows >= pulse_trains[1], 0.7, 1.0)
    amplitude = jnp.sqrt(2.0 * decay_rate / (1.0 - jnp.exp(-2.0 * decay_rate * FILTER_LENGTH)))
    noise = jnp.clip(jax.random.normal(complete_keys[4], (FILTER_LENGTH, FILTERS), jnp.float32), -4.0, 4.0)
    return jnp.clip(amplitude * decay_profile * noise, -1.0, 1.0).astype(jnp.bfloat16)


def block_levels(key, extent, shards, least, top_value):
    level = 1.0
    for axis_at, blocks in shards:
        steps = jax.random.uniform(jax.random.fold_in(jax.random.fold_in(key, 6), axis_at), (blocks,), jnp.float32, least / len(shards), top_value / len(shards))
        level = level * jnp.repeat(jnp.exp(steps), extent[axis_at] // blocks).reshape((-1,) + (1,) * (len(extent) - 1 - axis_at))
    return level


def scatter_about(rng, extent, width, reach, pieces=(), kind=jnp.bfloat16):
    factor_of = block_levels(rng, extent, pieces, -0.22, 0.18) if pieces else 1.0
    values = jax.random.normal(rng, extent, jnp.float32) * width * factor_of
    return jnp.minimum(jnp.maximum(values, -reach), reach).astype(kind)


def setup_inputs(seed: int = 0) -> dict:
    seeds = jax.random.split(jax.random.key(seed), 5)
    features = scatter_about(seeds[0], (BATCH, SEQ, 3 * CHANNELS), 1.0, 6.0, ((0, 16), (1, 16)))
    short_weight = scatter_about(seeds[1], (TAPS, 3 * CHANNELS), TAPS ** -0.5, 2.0, ((1, 16),))
    long_filter = draw_long_filter(jax.random.fold_in(seeds[4], 71), 0)
    out_weight = scatter_about(seeds[3], (CHANNELS, OUT_WIDTH), CHANNELS ** -0.5, 0.09375, ((1, 16),))
    return {"features": features, "short_weight": short_weight, "long_filter": long_filter, "out_weight": out_weight}


def brief_filter(sequence, short_weight):
    length = sequence.shape[0]
    padded = jnp.pad(sequence.astype(jnp.float32), ((TAPS - 1, 0), (0, 0)))
    weight_tensor = short_weight.astype(jnp.float32)
    result = jnp.zeros(sequence.shape, jnp.float32)
    for tap_index in range(TAPS):
        begin = TAPS - 1 - tap_index
        result = result + weight_tensor[tap_index] * padded[begin:begin + length]
    return result


def reference(features, short_weight, long_filter, out_weight):
    fft_length = 2 * SEQ
    filter_spectrum = jnp.fft.rfft(long_filter.astype(jnp.float32), n=fft_length, axis=0)
    filter_spectrum = jnp.tile(filter_spectrum, (1, CHANNELS // FILTERS))

    def one_sequence(sequence):
        filtered = brief_filter(sequence, short_weight)
        query = filtered[:, :CHANNELS]
        keys = filtered[:, CHANNELS:2 * CHANNELS]
        values = filtered[:, 2 * CHANNELS:]
        product = (keys * values).astype(jnp.bfloat16)
        product = lax.optimization_barrier(product).astype(jnp.float32)
        spectrum = jnp.fft.rfft(product, n=fft_length, axis=0) * filter_spectrum
        convolved = jnp.fft.irfft(spectrum, n=fft_length, axis=0)[:SEQ]
        gated = (query * convolved).astype(jnp.bfloat16)
        return jnp.dot(gated, out_weight, preferred_element_type=jnp.float32).astype(jnp.bfloat16)

    return lax.map(one_sequence, features)
```

```python
import functools

import jax
import jax.numpy as jnp
import ml_dtypes
import numpy as np
from jax import lax
from jax.experimental import pallas as pl
from jax.experimental.pallas import tpu as pltpu
from jax.sharding import PartitionSpec as P

MESH = pl.DeviceIdType.MESH
BF16 = jnp.bfloat16
F32 = jnp.float32

ROWS = 128
CHANNELS = 4096
FILTERS = 256
TAPS = 7
SPAN = 512
HALO = 16
PEERS = 4
CHUNKS = 4
WIDTH = CHANNELS // (PEERS * CHUNKS)
CHUNK = PEERS * WIDTH
SHARDS = 16
COLS = CHANNELS // SHARDS
OUT = PEERS * COLS
TAPCOLS = 3 * CHANNELS // SHARDS


def transform_matrices():
    order = np.concatenate([np.arange(0, SPAN, 2), np.arange(1, SPAN, 2)])
    turns = (np.outer(2 * order + 1, np.arange(SPAN)) % (4 * SPAN)) * (2 * np.pi / (4 * SPAN))
    forward = np.concatenate([np.cos(turns), -np.sin(turns)], axis=0)
    high = forward.astype(ml_dtypes.bfloat16)
    low = (forward - high.astype(np.float64)).astype(ml_dtypes.bfloat16)
    scale = np.float64(1.0 / SPAN)
    back_high = (high.astype(np.float64).T * scale).astype(ml_dtypes.bfloat16)
    back_low = (low.astype(np.float64).T * scale).astype(ml_dtypes.bfloat16)
    return high, low, back_high, back_low


def dot(a, b):
    return jnp.dot(a, b, preferred_element_type=F32)


def mixer_kernel(
    feat, taps_in, filt, weight, fwd_hi_in, fwd_lo_in, inv_hi_in, inv_lo_in,
    out,
    ext, taps_all, taps, fwd_hi, fwd_lo, inv_hi, inv_lo, spec, y_hi, y_lo,
    prod, cur, prev, convs, back, gated, wts, acc, outs,
    local_sem, halo_sem, tap_send, tap_recv, zf_send, zf_recv, yf_sem, zb_send, zb_recv,
    xg_send, xg_recv, wz_send, wz_recv, wy_send, wy_recv, wm_sem, wc_send, wc_recv, o_send, o_recv,
):
    ctx, fsdp = lax.axis_index("ctx"), lax.axis_index("fsdp")
    y, zl = ctx // 4, ctx % 4
    x, zh, core = fsdp // 4, (fsdp // 2) % 2, fsdp % 2
    slot = zh * 2 + core
    far_slot = (1 - zh) * 2 + core

    def device(y_=y, zl_=zl, x_=x, zh_=zh, core_=core):
        return (y_ * 4 + zl_, (x_ * 2 + zh_) * 2 + core_)

    def remote(src, dst, send, recv, to):
        return pltpu.make_async_remote_copy(
            src_ref=src, dst_ref=dst, send_sem=send, recv_sem=recv, device_id=to, device_id_type=MESH
        )

    def ring(k, at):
        return lax.rem(at + k, PEERS)

    loads = [
        pltpu.make_async_copy(feat, ext.at[pl.ds(HALO, ROWS)], local_sem.at[0]),
        pltpu.make_async_copy(taps_in, taps_all.at[fsdp], local_sem.at[1]),
        pltpu.make_async_copy(fwd_hi_in, fwd_hi, local_sem.at[2]),
        pltpu.make_async_copy(fwd_lo_in, fwd_lo, local_sem.at[3]),
        pltpu.make_async_copy(inv_hi_in, inv_hi, local_sem.at[4]),
        pltpu.make_async_copy(inv_lo_in, inv_lo, local_sem.at[5]),
        pltpu.make_async_copy(weight, wts.at[slot], local_sem.at[6]),
    ]
    for load in loads:
        load.start()

    barrier = pltpu.get_barrier_semaphore()

    def greet(to):
        pl.semaphore_signal(barrier, inc=1, device_id=to, device_id_type=MESH)

    def greet_shard(k, carry):
        greet((ctx, lax.rem(fsdp + k, SHARDS)))
        return carry

    lax.fori_loop(1, SHARDS, greet_shard, 0)
    for k in range(1, PEERS):
        greet(device(zl_=ring(k, zl)))
        greet(device(y_=ring(k, y)))
    after, before = lax.rem(ctx + 1, 16), lax.rem(ctx + 15, 16)
    greet((after, fsdp))
    greet((before, fsdp))
    greet(device(zl_=3 - zl, zh_=1 - zh))
    greet(device(zl_=ring(2, zl), zh_=1 - zh))
    pl.semaphore_wait(barrier, SHARDS - 1 + 2 * (PEERS - 1) + 4)

    halo = remote(feat.at[pl.ds(ROWS - HALO, HALO)], ext.at[pl.ds(0, HALO)], halo_sem.at[0], halo_sem.at[1], (after, fsdp))
    halo.start()

    def tap_copy(k):
        to = lax.rem(fsdp + k, SHARDS)
        return remote(taps_in, taps_all.at[fsdp], tap_send.at[k], tap_recv.at[fsdp], (ctx, to))

    def tap_arrival(k):
        peer = lax.rem(fsdp + k, SHARDS)
        return remote(taps_in, taps_all.at[peer], tap_send.at[k], tap_recv.at[peer], (ctx, peer))

    def start_taps(k, carry):
        tap_copy(k).start()
        return carry

    lax.fori_loop(1, SHARDS, start_taps, 0)

    def quarter(ref, which):
        return ref.at[pl.ds(pl.multiple_of(which * SPAN * 2, SPAN * 2), SPAN * 2)]

    mate = device(core_=1 - core)
    mate_copy = remote(weight, wts.at[slot], wm_sem.at[0], wm_sem.at[1], mate)
    mate_copy.start()

    def far_copy(j, to_zl):
        return remote(quarter(weight, y), quarter(wts.at[slot], y), wz_send.at[j], wz_recv, device(zl_=to_zl, zh_=1 - zh))

    @pl.when(zl == 0)
    def _():
        far_copy(0, 3).start()
        far_copy(1, 2).start()

    @pl.when(zl == 3)
    def _():
        far_copy(0, 0).start()
        far_copy(1, 1).start()

    for at in (2, 3):
        loads[at].wait()
    for part in range(4):
        rows = pl.ds(part * 256, 256)
        spec[rows, :] = dot(fwd_hi[rows, :], filt[...]) + dot(fwd_lo[rows, :], filt[...])

    loads[0].wait()
    loads[1].wait()
    halo.wait_recv()

    @pl.when(ctx == 0)
    def _():
        ext[pl.ds(0, HALO), :] = jnp.zeros((HALO, 3 * CHANNELS), BF16)

    @pl.when(y == 0)
    def _():
        prev[...] = jnp.zeros(prev.shape, BF16)

    def wait_taps(k, carry):
        tap_arrival(k).wait_recv()
        return carry

    lax.fori_loop(1, SHARDS, wait_taps, 0)
    for shard in range(SHARDS):
        block = taps_all[shard].astype(F32)
        taps[:, pl.ds(shard * TAPCOLS, TAPCOLS // 2)] = block[:8]
        taps[:, pl.ds(shard * TAPCOLS + TAPCOLS // 2, TAPCOLS // 2)] = block[8:]

    def short_filter(begin):
        columns = pl.ds(pl.multiple_of(begin, 128), 128)
        rows = ext[:, columns].astype(F32)
        weights = taps[:, columns]
        total = weights[0:1] * rows[HALO:]
        for lag in range(1, TAPS):
            total = total + weights[lag : lag + 1] * pltpu.roll(rows, lag, 0)[HALO:]
        return total

    def zf_copy(i, k):
        q = ring(k, zl)
        return remote(
            prod.at[i, q], cur.at[i, pl.ds(pl.multiple_of(zl * ROWS, ROWS), ROWS)], zf_send.at[i, k], zf_recv.at[i, zl], device(zl_=q)
        )

    def zf_arrival(i, k):
        q = ring(k, zl)
        return remote(
            prod.at[i, q], cur.at[i, pl.ds(pl.multiple_of(q * ROWS, ROWS), ROWS)], zf_send.at[i, k], zf_recv.at[i, q], device(zl_=q)
        )

    def products(i, carry):
        def one(q, inner):
            for part in range(WIDTH // 128):
                begin = i * CHUNK + q * WIDTH + part * 128
                keys = short_filter(CHANNELS + begin)
                values = short_filter(2 * CHANNELS + begin)
                prod[i, q, :, part * 128 : (part + 1) * 128] = (keys * values).astype(BF16)
            return inner

        lax.fori_loop(0, PEERS, one, 0)
        for k in range(1, PEERS):
            zf_copy(i, k).start()
        cur[i, pl.ds(pl.multiple_of(zl * ROWS, ROWS), ROWS), :] = prod[i, zl]
        return carry

    lax.fori_loop(0, CHUNKS, products, 0)

    def yf_copy(i):
        return remote(cur.at[i], prev.at[i], yf_sem.at[0, i], yf_sem.at[1, i], device(y_=ring(1, y)))

    def onward(i):
        for k in range(1, PEERS):
            zf_arrival(i, k).wait_recv()

        @pl.when(y < PEERS - 1)
        def _():
            yf_copy(i).start()

    def zb_copy(i, k):
        q = ring(k, zl)
        return remote(
            convs.at[i, pl.ds(pl.multiple_of(q * ROWS, ROWS), ROWS)], back.at[i, zl], zb_send.at[i, k], zb_recv.at[i, zl], device(zl_=q)
        )

    def zb_arrival(i, k):
        q = ring(k, zl)
        return remote(
            convs.at[i, pl.ds(pl.multiple_of(q * ROWS, ROWS), ROWS)], back.at[i, q], zb_send.at[i, k], zb_recv.at[i, q], device(zl_=q)
        )

    def convolve(i):
        @pl.when(y > 0)
        def _():
            yf_copy(i).wait_recv()

        def frequencies(part, carry):
            real = pl.ds(pl.multiple_of(part * 128, 128), 128)
            imag = pl.ds(pl.multiple_of(SPAN + part * 128, 128), 128)
            new, old = cur[i], prev[i]
            cr = dot(fwd_hi[real, :], new) + dot(fwd_lo[real, :], new)
            ci = dot(fwd_hi[imag, :], new) + dot(fwd_lo[imag, :], new)
            pr = dot(fwd_hi[real, :], old) + dot(fwd_lo[real, :], old)
            pi = dot(fwd_hi[imag, :], old) + dot(fwd_lo[imag, :], old)
            sign = jnp.where(part < 2, 1.0, -1.0).astype(F32)
            a = cr - sign * pi
            b = ci + sign * pr
            hr, hi = spec[real, :], spec[imag, :]
            yr = hr * a - hi * b
            yi = hr * b + hi * a
            yr_hi, yi_hi = yr.astype(BF16), yi.astype(BF16)
            y_hi[real, :] = yr_hi
            y_hi[imag, :] = yi_hi
            y_lo[real, :] = (yr - yr_hi.astype(F32)).astype(BF16)
            y_lo[imag, :] = (yi - yi_hi.astype(F32)).astype(BF16)
            return carry

        lax.fori_loop(0, 4, frequencies, 0)

        def positions(part, carry):
            rows = pl.ds(pl.multiple_of(part * ROWS, ROWS), ROWS)
            got = dot(inv_hi[rows, :], y_hi[...]) + dot(inv_hi[rows, :], y_lo[...]) + dot(inv_lo[rows, :], y_hi[...])
            convs[i, rows, :] = got.astype(BF16)
            return carry

        lax.fori_loop(0, PEERS, positions, 0)
        for k in range(1, PEERS):
            zb_copy(i, k).start()
        back[i, zl] = convs[i, pl.ds(pl.multiple_of(zl * ROWS, ROWS), ROWS), :]

    def xg_copy(i, k):
        return remote(gated.at[i, x], gated.at[i, x], xg_send.at[i, k], xg_recv.at[i, x], device(x_=ring(k, x)))

    def xg_arrival(i, k):
        q = ring(k, x)
        return remote(gated.at[i, q], gated.at[i, q], xg_send.at[i, k], xg_recv.at[i, q], device(x_=q))

    def gate(i):
        for k in range(1, PEERS):
            zb_arrival(i, k).wait_recv()
        for q in range(PEERS):
            for part in range(WIDTH // 128):
                lanes = slice(part * 128, (part + 1) * 128)
                query = short_filter(i * CHUNK + q * WIDTH + part * 128)
                gated[i, x, :, q * WIDTH + part * 128 : q * WIDTH + (part + 1) * 128] = (query * back[i, q, :, lanes].astype(F32)).astype(BF16)
        for k in range(1, PEERS):
            xg_copy(i, k).start()

    def project(i):
        for k in range(1, PEERS):
            xg_arrival(i, k).wait_recv()
        lhs = gated[i].reshape(PEERS * ROWS, CHUNK)

        def block(j, carry):
            term = dot(lhs, wts[j, pl.ds(pl.multiple_of(i * CHUNK, CHUNK), CHUNK), :])

            @pl.when(i == 0)
            def _():
                acc[j] = term

            @pl.when(i > 0)
            def _():
                acc[j] = acc[j] + term

            return carry

        lax.fori_loop(0, PEERS, block, 0)

    def wy_copy(k):
        ref = quarter(wts.at[far_slot], y)
        return remote(ref, ref, wy_send.at[k], wy_recv.at[y], device(y_=ring(k, y)))

    def wy_arrival(k):
        ref = quarter(wts.at[far_slot], ring(k, y))
        return remote(ref, ref, wy_send.at[k], wy_recv.at[ring(k, y)], device(y_=ring(k, y)))

    def wc_copy(which):
        ref = quarter(wts.at[far_slot], which)
        return remote(ref, ref, wc_send.at[which], wc_recv.at[which], mate)

    def wc_arrival(which):
        ref = quarter(wts.at[(1 - zh) * 2 + 1 - core], which)
        return remote(ref, ref, wc_send.at[which], wc_recv.at[which], mate)

    def columns_first():
        far = quarter(wts.at[far_slot], y)
        remote(far, far, wz_send.at[0], wz_recv, device(zl_=3 - zl, zh_=1 - zh)).wait_recv()
        for k in range(1, PEERS):
            wy_copy(k).start()
        wc_copy(y).start()

    def columns_rest():
        for k in range(1, PEERS):
            wy_arrival(k).wait_recv()
            wc_copy(ring(k, y)).start()

    def columns_last():
        loads[6].wait()
        mate_copy.wait_recv()
        for which in range(PEERS):
            wc_arrival(which).wait_recv()

    for at in (4, 5):
        loads[at].wait()

    def step(t, carry):
        @pl.when(t < CHUNKS)
        def _():
            onward(t)

        @pl.when(jnp.logical_and(t >= 1, t < CHUNKS + 1))
        def _():
            convolve(t - 1)

        @pl.when(t == 1)
        def _():
            columns_first()

        @pl.when(jnp.logical_and(t >= 2, t < CHUNKS + 2))
        def _():
            gate(t - 2)

        @pl.when(t == 3)
        def _():
            columns_rest()
            columns_last()

        @pl.when(t >= 3)
        def _():
            project(t - 3)

        return carry

    lax.fori_loop(0, CHUNKS + 3, step, 0)

    mine = pl.ds(pl.multiple_of(x * OUT, OUT), OUT)

    def out_copy(k):
        q = ring(k, x)
        return remote(outs.at[q], out.at[:, mine], o_send.at[k], o_recv.at[x], device(x_=q))

    def out_arrival(k):
        q = ring(k, x)
        return remote(outs.at[q], out.at[:, pl.ds(pl.multiple_of(q * OUT, OUT), OUT)], o_send.at[k], o_recv.at[q], device(x_=q))

    def finish(q, carry):
        for j in range(PEERS):
            outs[q, :, j * COLS : (j + 1) * COLS] = acc[j, pl.ds(pl.multiple_of(q * ROWS, ROWS), ROWS), :].astype(BF16)
        return carry

    lax.fori_loop(0, PEERS, finish, 0)
    for k in range(1, PEERS):
        out_copy(k).start()
    own = pltpu.make_async_copy(outs.at[x], out.at[:, mine], local_sem.at[7])
    own.start()
    own.wait()
    for k in range(1, PEERS):
        out_arrival(k).wait_recv()

    halo.wait_send()
    mate_copy.wait_send()

    def sent_taps(k, carry):
        tap_copy(k).wait_send()
        return carry

    lax.fori_loop(1, SHARDS, sent_taps, 0)

    @pl.when(jnp.logical_or(zl == 0, zl == 3))
    def _():
        far_copy(0, 3 - zl).wait_send()
        far_copy(1, ring(2, zl)).wait_send()

    for k in range(1, PEERS):
        wy_copy(k).wait_send()
        out_copy(k).wait_send()
    for which in range(PEERS):
        wc_copy(which).wait_send()

    def sent_chunk(i, carry):
        for k in range(1, PEERS):
            zf_copy(i, k).wait_send()
            zb_copy(i, k).wait_send()
            xg_copy(i, k).wait_send()

        @pl.when(y < PEERS - 1)
        def _():
            yf_copy(i).wait_send()

        return carry

    lax.fori_loop(0, CHUNKS, sent_chunk, 0)


def shards(features, short_weight, long_filter, out_weight):
    padded = jnp.pad(short_weight, ((0, 8 - TAPS), (0, 0)))
    packed = jnp.concatenate([padded[:, : TAPCOLS // 2], padded[:, TAPCOLS // 2 :]], axis=0)
    matrices = [jnp.asarray(m) for m in transform_matrices()]
    anywhere = pl.BlockSpec(memory_space=pl.ANY)
    dma = pltpu.SemaphoreType.DMA
    result = pl.pallas_call(
        mixer_kernel,
        name="mixer",
        out_shape=jax.ShapeDtypeStruct((ROWS, CHANNELS), BF16),
        in_specs=[anywhere, anywhere, pl.BlockSpec(memory_space=pltpu.VMEM)] + [anywhere] * 5,
        out_specs=anywhere,
        scratch_shapes=[
            pltpu.VMEM((HALO + ROWS, 3 * CHANNELS), BF16),
            pltpu.VMEM((SHARDS, 16, TAPCOLS // 2), BF16),
            pltpu.VMEM((8, 3 * CHANNELS), F32),
            pltpu.VMEM((2 * SPAN, SPAN), BF16),
            pltpu.VMEM((2 * SPAN, SPAN), BF16),
            pltpu.VMEM((SPAN, 2 * SPAN), BF16),
            pltpu.VMEM((SPAN, 2 * SPAN), BF16),
            pltpu.VMEM((2 * SPAN, FILTERS), F32),
            pltpu.VMEM((2 * SPAN, WIDTH), BF16),
            pltpu.VMEM((2 * SPAN, WIDTH), BF16),
            pltpu.VMEM((CHUNKS, PEERS, ROWS, WIDTH), BF16),
            pltpu.VMEM((CHUNKS, SPAN, WIDTH), BF16),
            pltpu.VMEM((CHUNKS, SPAN, WIDTH), BF16),
            pltpu.VMEM((CHUNKS, SPAN, WIDTH), BF16),
            pltpu.VMEM((CHUNKS, PEERS, ROWS, WIDTH), BF16),
            pltpu.VMEM((CHUNKS, PEERS, ROWS, CHUNK), BF16),
            pltpu.VMEM((PEERS, CHANNELS, COLS), BF16),
            pltpu.VMEM((PEERS, PEERS * ROWS, COLS), F32),
            pltpu.VMEM((PEERS, ROWS, OUT), BF16),
            dma((8,)), dma((2,)), dma((SHARDS,)), dma((SHARDS,)),
            dma((CHUNKS, PEERS)), dma((CHUNKS, PEERS)), dma((2, CHUNKS)), dma((CHUNKS, PEERS)), dma((CHUNKS, PEERS)),
            dma((CHUNKS, PEERS)), dma((CHUNKS, PEERS)), dma((2,)), dma, dma((PEERS,)), dma((PEERS,)),
            dma((2,)), dma((PEERS,)), dma((PEERS,)), dma((PEERS,)), dma((PEERS,)),
        ],
        compiler_params=pltpu.CompilerParams(collective_id=0, has_side_effects=True, vmem_limit_bytes=56 * 2**20),
    )(features[0], packed, long_filter, out_weight, *matrices)
    return result[None]


def solution(mesh):
    placed = (P("fsdp", "ctx", None), P(None, "fsdp"), P(), P(None, "fsdp"))
    return jax.shard_map(
        shards, mesh=mesh, in_specs=placed, out_specs=P("fsdp", "ctx", None), check_vma=False
    )
```

```python
import functools

import jax
import jax.numpy as jnp
import ml_dtypes
import numpy as np
from jax import lax
from jax.experimental import pallas as pl
from jax.experimental.pallas import tpu as pltpu
from jax.sharding import PartitionSpec as P

MESH = pl.DeviceIdType.MESH
BF16 = jnp.bfloat16
F32 = jnp.float32

ROWS = 128
CHANNELS = 4096
FILTERS = 256
TAPS = 7
SPAN = 512
HALO = 8
PEERS = 4
CHUNKS = 8
GROUPS = 4
WIDTH = CHANNELS // (PEERS * CHUNKS)
CHUNK = PEERS * WIDTH
GROUP = CHANNELS // GROUPS
HALF = GROUP // 2
NEAR = 8
SHARDS = 16
COLS = CHANNELS // SHARDS
OUT = PEERS * COLS
TAPCOLS = 3 * CHANNELS // SHARDS


def transform_matrices():
    order = np.concatenate([np.arange(0, SPAN, 2), np.arange(1, SPAN, 2)])
    turns = (np.outer(2 * order + 1, np.arange(SPAN)) % (4 * SPAN)) * (2 * np.pi / (4 * SPAN))
    forward = np.concatenate([np.cos(turns), -np.sin(turns)], axis=0)
    high = forward.astype(ml_dtypes.bfloat16)
    low = (forward - high.astype(np.float64)).astype(ml_dtypes.bfloat16)
    scale = np.float64(1.0 / SPAN)
    back_high = (high.astype(np.float64).T * scale).astype(ml_dtypes.bfloat16)
    back_low = (low.astype(np.float64).T * scale).astype(ml_dtypes.bfloat16)
    return high, low, back_high, back_low


def dot(a, b):
    return jnp.dot(a, b, preferred_element_type=F32)


def mixer_kernel(
    feat, taps_in, filt, weight, fwd_hi_in, fwd_lo_in, inv_hi_in, inv_lo_in,
    out,
    ext, tail, halo_out, halo_in, halo, taps_all, taps, fwd_hi, fwd_lo, inv_hi, inv_lo, spec, y_hi, y_lo,
    prod, cur, prev, convs, back, gated, wts, acc, outs,
    local_sem, halo_send, halo_recv, tap_send, tap_recv, zf_send, zf_recv, yf_sem, zb_send, zb_recv,
    xg_send, xg_recv, xr_send, xr_recv, wz_send, wz_recv, wy_send, wy_recv, wm_sem, wc_send, wc_recv, o_send, o_recv,
):
    ctx, fsdp = lax.axis_index("ctx"), lax.axis_index("fsdp")
    y, zl = ctx // 4, ctx % 4
    x, zh, core = fsdp // 4, (fsdp // 2) % 2, fsdp % 2
    slot = zh * 2 + core
    far_slot = (1 - zh) * 2 + core
    far_shard = x * 4 + far_slot

    def device(y_=y, zl_=zl, x_=x, zh_=zh, core_=core):
        return (y_ * 4 + zl_, (x_ * 2 + zh_) * 2 + core_)

    def remote(src, dst, send, recv, to):
        return pltpu.make_async_remote_copy(
            src_ref=src, dst_ref=dst, send_sem=send, recv_sem=recv, device_id=to, device_id_type=MESH
        )

    def ring(k, at):
        return lax.rem(at + k, PEERS)

    def features_load(part, at):
        lanes = pl.ds(part * CHANNELS, CHANNELS)
        return pltpu.make_async_copy(feat.at[:, lanes], ext.at[:, lanes], local_sem.at[at])

    tail_load = pltpu.make_async_copy(feat.at[pl.ds(ROWS - 16, 16)], tail, local_sem.at[9])
    tail_load.start()
    loads = [
        features_load(1, 0),
        features_load(2, 1),
        pltpu.make_async_copy(fwd_hi_in, fwd_hi, local_sem.at[2]),
        pltpu.make_async_copy(fwd_lo_in, fwd_lo, local_sem.at[3]),
        features_load(0, 4),
        pltpu.make_async_copy(inv_hi_in, inv_hi, local_sem.at[5]),
        pltpu.make_async_copy(inv_lo_in, inv_lo, local_sem.at[6]),
        pltpu.make_async_copy(weight, wts.at[slot], local_sem.at[7]),
    ]
    for load in loads:
        load.start()

    barrier = pltpu.get_barrier_semaphore()

    def greet(to):
        pl.semaphore_signal(barrier, inc=1, device_id=to, device_id_type=MESH)

    def near(k):
        other = lax.rem(x * 2 + core + k, NEAR)
        return other // 2, lax.rem(other, 2)

    def greet_near(k, carry):
        x_, core_ = near(k)
        greet(device(x_=x_, core_=core_))
        return carry

    lax.fori_loop(1, NEAR, greet_near, 0)
    for k in range(1, PEERS):
        greet(device(zl_=ring(k, zl)))
        greet(device(y_=ring(k, y)))
    after, before = lax.rem(ctx + 1, 16), lax.rem(ctx + 15, 16)
    greet((after, fsdp))
    greet((before, fsdp))
    greet(device(zh_=1 - zh))
    greet(device(zl_=3 - zl, zh_=1 - zh))
    greet(device(zl_=ring(2, zl), zh_=1 - zh))

    own_taps = jnp.concatenate([taps_in[...].astype(F32), jnp.zeros((8 - TAPS, TAPCOLS), F32)], axis=0)
    own_taps = jnp.concatenate([own_taps[:, : TAPCOLS // 2], own_taps[:, TAPCOLS // 2 :]], axis=0)
    taps_all[fsdp] = own_taps.astype(BF16)

    tail_load.wait()

    def pack(part, group):
        rows = tail[:, part * CHANNELS + group * GROUP : part * CHANNELS + (group + 1) * GROUP].astype(F32)[16 - HALO :]
        packed = jnp.concatenate([rows[:, :HALF], rows[:, HALF:]], axis=0)
        return packed.astype(BF16)

    for group in range(GROUPS):
        halo_out[group, 0] = pack(1, group)
        halo_out[group, 1] = pack(2, group)
        halo_out[GROUPS + group // 2, group % 2] = pack(0, group)

    pl.semaphore_wait(barrier, NEAR - 1 + 2 * (PEERS - 1) + 5)

    far_taps = remote(taps_all.at[fsdp], taps_all.at[fsdp], tap_send.at[0, 0], tap_recv.at[fsdp], device(zh_=1 - zh))
    far_taps.start()

    def tap_copy(k, zh_):
        x_, core_ = near(k)
        shard = x * 4 + zh_ * 2 + core
        return remote(taps_all.at[shard], taps_all.at[shard], tap_send.at[zh_, k], tap_recv.at[shard], device(x_=x_, core_=core_))

    def tap_arrival(k, zh_):
        x_, core_ = near(k)
        shard = x_ * 4 + zh_ * 2 + core_
        return remote(taps_all.at[shard], taps_all.at[shard], tap_send.at[zh_, k], tap_recv.at[shard], device(x_=x_, core_=core_))

    def start_taps(k, carry):
        tap_copy(k, zh).start()
        return carry

    lax.fori_loop(1, NEAR, start_taps, 0)

    def halo_copy(at):
        return remote(halo_out.at[at], halo_in.at[at], halo_send.at[at], halo_recv.at[at], (after, fsdp))

    for group in range(GROUPS):
        halo_copy(group).start()

    def quarter(ref, which):
        return ref.at[pl.ds(pl.multiple_of(which * GROUP, GROUP), GROUP)]

    mate = device(core_=1 - core)
    mate_copy = remote(weight, wts.at[slot], wm_sem.at[0], wm_sem.at[1], mate)
    mate_copy.start()

    def far_copy(j, to_zl):
        return remote(quarter(weight, y), quarter(wts.at[slot], y), wz_send.at[j], wz_recv, device(zl_=to_zl, zh_=1 - zh))

    @pl.when(zl == 0)
    def _():
        far_copy(1, 2).start()
        far_copy(0, 3).start()

    @pl.when(zl == 3)
    def _():
        far_copy(1, 1).start()
        far_copy(0, 0).start()

    remote(taps_all.at[far_shard], taps_all.at[far_shard], tap_send.at[0, 0], tap_recv.at[far_shard], device(zh_=1 - zh)).wait_recv()

    def pass_taps(k, carry):
        tap_copy(k, 1 - zh).start()
        return carry

    lax.fori_loop(1, NEAR, pass_taps, 0)

    loads[2].wait()
    loads[3].wait()
    mine_filt = filt[:, pl.ds(pl.multiple_of(lax.rem(zl, FILTERS // WIDTH) * WIDTH, WIDTH), WIDTH)]
    for part in range(4):
        rows = pl.ds(part * 256, 256)
        spec[rows, :] = dot(fwd_hi[rows, :], mine_filt) + dot(fwd_lo[rows, :], mine_filt)

    @pl.when(y == 0)
    def _():
        prev[...] = jnp.zeros(prev.shape, BF16)

    loads[0].wait()
    loads[1].wait()
    loads[4].wait()

    def wait_taps(k, carry):
        tap_arrival(k, 0).wait_recv()
        tap_arrival(k, 1).wait_recv()
        return carry

    lax.fori_loop(1, NEAR, wait_taps, 0)
    for shard in range(SHARDS):
        block = taps_all[shard].astype(F32)
        taps[:, pl.ds(shard * TAPCOLS, TAPCOLS // 2)] = block[:8]
        taps[:, pl.ds(shard * TAPCOLS + TAPCOLS // 2, TAPCOLS // 2)] = block[8:]

    keep = jnp.where(ctx > 0, 1.0, 0.0).astype(F32)

    def unpack(at, which, begin):
        block = halo_in[at, which].astype(F32) * keep
        halo[:, pl.ds(pl.multiple_of(begin, HALF), HALF)] = block[:HALO]
        halo[:, pl.ds(pl.multiple_of(begin + HALF, HALF), HALF)] = block[HALO:]

    def short_filter(begin):
        columns = pl.ds(pl.multiple_of(begin, 128), 128)
        rows = jnp.concatenate([halo[:, columns], ext[:, columns].astype(F32)], axis=0)
        weights = taps[:, columns]
        total = weights[0:1] * rows[HALO:]
        for lag in range(1, TAPS):
            total = total + weights[lag : lag + 1] * pltpu.roll(rows, lag, 0)[HALO:]
        return total

    def own_rows(which):
        return pl.ds(pl.multiple_of(which * ROWS, ROWS), ROWS)

    def zf_copy(i, k):
        q = ring(k, zl)
        return remote(prod.at[i, q], cur.at[i, own_rows(zl)], zf_send.at[i, k], zf_recv.at[i, zl], device(zl_=q))

    def zf_arrival(i, k):
        q = ring(k, zl)
        return remote(prod.at[i, q], cur.at[i, own_rows(q)], zf_send.at[i, k], zf_recv.at[i, q], device(zl_=q))

    def products(i):
        group = i // 2

        @pl.when(lax.rem(i, 2) == 0)
        def _():
            halo_copy(group).wait_recv()
            unpack(group, 0, CHANNELS + group * GROUP)
            unpack(group, 1, 2 * CHANNELS + group * GROUP)

        def one(q, inner):
            begin = i * CHUNK + q * WIDTH
            keys = short_filter(CHANNELS + begin)
            values = short_filter(2 * CHANNELS + begin)
            prod[i, q] = (keys * values).astype(BF16)
            return inner

        lax.fori_loop(0, PEERS, one, 0)
        for k in range(1, PEERS):
            zf_copy(i, k).start()
        cur[i, own_rows(zl), :] = prod[i, zl]

        @pl.when(i == 1)
        def _():
            for at in (GROUPS, GROUPS + 1):
                halo_copy(at).start()


    def yf_copy(i):
        return remote(cur.at[i], prev.at[i], yf_sem.at[0, i], yf_sem.at[1, i], device(y_=ring(1, y)))

    def onward(i):
        for k in range(1, PEERS):
            zf_arrival(i, k).wait_recv()

        @pl.when(y < PEERS - 1)
        def _():
            yf_copy(i).start()

    def zb_copy(i, k):
        q = ring(k, zl)
        return remote(convs.at[i, own_rows(q)], back.at[i, zl], zb_send.at[i, k], zb_recv.at[i, zl], device(zl_=q))

    def zb_arrival(i, k):
        q = ring(k, zl)
        return remote(convs.at[i, own_rows(q)], back.at[i, q], zb_send.at[i, k], zb_recv.at[i, q], device(zl_=q))

    def convolve(i):
        @pl.when(y > 0)
        def _():
            yf_copy(i).wait_recv()

        def frequencies(part, carry):
            real = pl.ds(pl.multiple_of(part * 128, 128), 128)
            imag = pl.ds(pl.multiple_of(SPAN + part * 128, 128), 128)
            both = jnp.concatenate([cur[i], prev[i]], axis=1)
            re = dot(fwd_hi[real, :], both) + dot(fwd_lo[real, :], both)
            im = dot(fwd_hi[imag, :], both) + dot(fwd_lo[imag, :], both)
            sign = jnp.where(part < 2, 1.0, -1.0).astype(F32)
            a = re[:, :WIDTH] - sign * im[:, WIDTH:]
            b = im[:, :WIDTH] + sign * re[:, WIDTH:]
            hr, hi = spec[real, :], spec[imag, :]
            yr = hr * a - hi * b
            yi = hr * b + hi * a
            yr_hi, yi_hi = yr.astype(BF16), yi.astype(BF16)
            y_hi[real, :] = yr_hi
            y_hi[imag, :] = yi_hi
            y_lo[real, :] = (yr - yr_hi.astype(F32)).astype(BF16)
            y_lo[imag, :] = (yi - yi_hi.astype(F32)).astype(BF16)
            return carry

        lax.fori_loop(0, 4, frequencies, 0)

        def positions(part, carry):
            rows = own_rows(part)
            both = dot(inv_hi[rows, :], jnp.concatenate([y_hi[...], y_lo[...]], axis=1))
            got = both[:, :WIDTH] + both[:, WIDTH:] + dot(inv_lo[rows, :], y_hi[...])
            convs[i, rows, :] = got.astype(BF16)
            return carry

        lax.fori_loop(0, PEERS, positions, 0)
        for k in range(1, PEERS):
            zb_copy(i, k).start()
        back[i, zl] = convs[i, own_rows(zl), :]

    left, right = ring(3, x), ring(1, x)

    def xg_copy(i, to, at):
        return remote(gated.at[i, x], gated.at[i, x], xg_send.at[i, at], xg_recv.at[i, x], device(x_=to))

    def xg_arrival(i, source, at):
        return remote(gated.at[i, source], gated.at[i, source], xg_send.at[i, at], xg_recv.at[i, source], device(x_=source))

    def xr_copy(i, source, to, at):
        ref = gated.at[i, source, pl.ds(at * (ROWS // 2), ROWS // 2)]
        return remote(ref, ref, xr_send.at[i, at], xr_recv.at[i, at], device(x_=to))

    def gate(i):
        @pl.when(i == 0)
        def _():
            for at in (GROUPS, GROUPS + 1):
                halo_copy(at).wait_recv()
            for group in range(GROUPS):
                unpack(GROUPS + group // 2, group % 2, group * GROUP)

        for k in range(1, PEERS):
            zb_arrival(i, k).wait_recv()
        for q in range(PEERS):
            query = short_filter(i * CHUNK + q * WIDTH)
            gated[i, x, :, q * WIDTH : (q + 1) * WIDTH] = (query * back[i, q].astype(F32)).astype(BF16)
        xg_copy(i, right, 0).start()
        xg_copy(i, left, 1).start()

    def relay(i):
        xg_arrival(i, left, 0).wait_recv()
        xr_copy(i, left, right, 0).start()
        xg_arrival(i, right, 1).wait_recv()
        xr_copy(i, right, left, 1).start()

    def far_arrivals(i):
        across = ring(2, x)
        xr_copy(i, across, left, 0).wait_recv()
        xr_copy(i, across, right, 1).wait_recv()

    def project(group):
        far_arrivals(2 * group)
        far_arrivals(2 * group + 1)
        lhs = [gated[2 * group + part].reshape(PEERS * ROWS, CHUNK) for part in range(2)]

        def block(j, carry):
            term = acc[j]
            for part in range(2):
                term = term + dot(lhs[part], wts[j, pl.ds(pl.multiple_of(group * GROUP + part * CHUNK, CHUNK), CHUNK), :])
            acc[j] = term
            return carry

        lax.fori_loop(0, PEERS, block, 0)

    def wy_copy(k):
        ref = quarter(wts.at[far_slot], ring(k, y))
        return remote(ref, ref, wy_send.at[k], wy_recv.at[k], device(y_=ring(3, y)))

    def wy_arrival(k):
        ref = quarter(wts.at[far_slot], ring(k + 1, y))
        return remote(ref, ref, wy_send.at[k], wy_recv.at[k], device(y_=ring(1, y)))

    def wc_copy(which):
        ref = quarter(wts.at[far_slot], which)
        return remote(ref, ref, wc_send.at[which], wc_recv.at[which], mate)

    def wc_arrival(which):
        ref = quarter(wts.at[(1 - zh) * 2 + 1 - core], which)
        return remote(ref, ref, wc_send.at[which], wc_recv.at[which], mate)

    def columns_first():
        far = quarter(wts.at[far_slot], y)
        remote(far, far, wz_send.at[0], wz_recv, device(zl_=3 - zl, zh_=1 - zh)).wait_recv()
        wy_copy(0).start()
        wc_copy(y).start()

    def columns_next(k):
        wy_arrival(k - 1).wait_recv()

        @pl.when(k < PEERS - 1)
        def _():
            wy_copy(k).start()

        wc_copy(ring(k, y)).start()

    def columns_last():
        loads[7].wait()
        mate_copy.wait_recv()
        for which in range(PEERS):
            wc_arrival(which).wait_recv()

    loads[5].wait()
    loads[6].wait()
    acc[...] = jnp.zeros(acc.shape, F32)

    def step(t, carry):
        @pl.when(t < CHUNKS)
        def _():
            products(t)

        @pl.when(jnp.logical_and(t >= 2, t < CHUNKS + 2))
        def _():
            onward(t - 2)

        @pl.when(jnp.logical_and(t >= 3, t < CHUNKS + 3))
        def _():
            convolve(t - 3)

        @pl.when(jnp.logical_and(t >= 4, t < CHUNKS + 4))
        def _():
            gate(t - 4)

        @pl.when(t >= 5)
        def _():
            relay(t - 5)

        @pl.when(t == 4)
        def _():
            columns_first()

        @pl.when(jnp.logical_or(t == 6, jnp.logical_or(t == 8, t == 10)))
        def _():
            columns_next(t // 2 - 2)

        @pl.when(t == 10)
        def _():
            columns_last()

        @pl.when(t >= 10)
        def _():
            project(t - 10)

        return carry

    lax.fori_loop(0, CHUNKS + 5, step, 0)

    mine = pl.ds(pl.multiple_of(x * OUT, OUT), OUT)

    def out_copy(k):
        q = ring(k, x)
        return remote(outs.at[q], out.at[:, mine], o_send.at[k], o_recv.at[x], device(x_=q))

    def out_arrival(k):
        q = ring(k, x)
        return remote(outs.at[q], out.at[:, pl.ds(pl.multiple_of(q * OUT, OUT), OUT)], o_send.at[k], o_recv.at[q], device(x_=q))

    last = GROUPS - 1
    far_arrivals(2 * last)
    far_arrivals(2 * last + 1)

    def finish(k, carry):
        q = ring(k, x)
        lhs = jnp.concatenate([gated[2 * last, q], gated[2 * last + 1, q]], axis=1)
        for j in range(PEERS):
            total = acc[j, own_rows(q), :] + dot(lhs, wts[j, last * GROUP :, :])
            outs[q, :, j * COLS : (j + 1) * COLS] = total.astype(BF16)

        @pl.when(k < PEERS)
        def _():
            out_copy(k).start()

        return carry

    lax.fori_loop(1, PEERS + 1, finish, 0)
    own = pltpu.make_async_copy(outs.at[x], out.at[:, mine], local_sem.at[8])
    own.start()
    own.wait()
    for k in range(1, PEERS):
        out_arrival(k).wait_recv()

    far_taps.wait_send()
    mate_copy.wait_send()
    for at in range(GROUPS + 2):
        halo_copy(at).wait_send()

    def sent_taps(k, carry):
        tap_copy(k, 0).wait_send()
        tap_copy(k, 1).wait_send()
        return carry

    lax.fori_loop(1, NEAR, sent_taps, 0)

    @pl.when(jnp.logical_or(zl == 0, zl == 3))
    def _():
        far_copy(0, 3 - zl).wait_send()
        far_copy(1, ring(2, zl)).wait_send()

    for k in range(1, PEERS):
        wy_copy(k - 1).wait_send()
        out_copy(k).wait_send()
    for which in range(PEERS):
        wc_copy(which).wait_send()

    def sent_chunk(i, carry):
        for k in range(1, PEERS):
            zf_copy(i, k).wait_send()
            zb_copy(i, k).wait_send()
        xg_copy(i, right, 0).wait_send()
        xg_copy(i, left, 1).wait_send()
        xr_copy(i, left, right, 0).wait_send()
        xr_copy(i, right, left, 1).wait_send()

        @pl.when(y < PEERS - 1)
        def _():
            yf_copy(i).wait_send()

        return carry

    lax.fori_loop(0, CHUNKS, sent_chunk, 0)


def shards(features, short_weight, long_filter, out_weight):
    matrices = [jnp.asarray(m) for m in transform_matrices()]
    anywhere = pl.BlockSpec(memory_space=pl.ANY)
    dma = pltpu.SemaphoreType.DMA
    result = pl.pallas_call(
        mixer_kernel,
        name="mixer",
        out_shape=jax.ShapeDtypeStruct((ROWS, CHANNELS), BF16),
        in_specs=[anywhere, pl.BlockSpec(memory_space=pltpu.VMEM), pl.BlockSpec(memory_space=pltpu.VMEM)] + [anywhere] * 5,
        out_specs=anywhere,
        scratch_shapes=[
            pltpu.VMEM((ROWS, 3 * CHANNELS), BF16),
            pltpu.VMEM((16, 3 * CHANNELS), BF16),
            pltpu.VMEM((GROUPS + 2, 2, 2 * HALO, HALF), BF16),
            pltpu.VMEM((GROUPS + 2, 2, 2 * HALO, HALF), BF16),
            pltpu.VMEM((HALO, 3 * CHANNELS), F32),
            pltpu.VMEM((SHARDS, 16, TAPCOLS // 2), BF16),
            pltpu.VMEM((8, 3 * CHANNELS), F32),
            pltpu.VMEM((2 * SPAN, SPAN), BF16),
            pltpu.VMEM((2 * SPAN, SPAN), BF16),
            pltpu.VMEM((SPAN, 2 * SPAN), BF16),
            pltpu.VMEM((SPAN, 2 * SPAN), BF16),
            pltpu.VMEM((2 * SPAN, WIDTH), F32),
            pltpu.VMEM((2 * SPAN, WIDTH), BF16),
            pltpu.VMEM((2 * SPAN, WIDTH), BF16),
            pltpu.VMEM((CHUNKS, PEERS, ROWS, WIDTH), BF16),
            pltpu.VMEM((CHUNKS, SPAN, WIDTH), BF16),
            pltpu.VMEM((CHUNKS, SPAN, WIDTH), BF16),
            pltpu.VMEM((CHUNKS, SPAN, WIDTH), BF16),
            pltpu.VMEM((CHUNKS, PEERS, ROWS, WIDTH), BF16),
            pltpu.VMEM((CHUNKS, PEERS, ROWS, CHUNK), BF16),
            pltpu.VMEM((PEERS, CHANNELS, COLS), BF16),
            pltpu.VMEM((PEERS, PEERS * ROWS, COLS), F32),
            pltpu.VMEM((PEERS, ROWS, OUT), BF16),
            dma((10,)), dma((GROUPS + 2,)), dma((GROUPS + 2,)), dma((2, NEAR)), dma((SHARDS,)),
            dma((CHUNKS, PEERS)), dma((CHUNKS, PEERS)), dma((2, CHUNKS)), dma((CHUNKS, PEERS)), dma((CHUNKS, PEERS)),
            dma((CHUNKS, 2)), dma((CHUNKS, PEERS)), dma((CHUNKS, 2)), dma((CHUNKS, 2)),
            dma((2,)), dma, dma((PEERS,)), dma((PEERS,)), dma((2,)), dma((PEERS,)), dma((PEERS,)), dma((PEERS,)), dma((PEERS,)),
        ],
        compiler_params=pltpu.CompilerParams(collective_id=0, has_side_effects=True, vmem_limit_bytes=56 * 2**20),
    )(features[0], short_weight, long_filter, out_weight, *matrices)
    return result[None]


def solution(mesh):
    placed = (P("fsdp", "ctx", None), P(None, "fsdp"), P(), P(None, "fsdp"))
    return jax.shard_map(
        shards, mesh=mesh, in_specs=placed, out_specs=P("fsdp", "ctx", None), check_vma=False
    )
```

```python
import functools

import jax
import jax.numpy as jnp
import ml_dtypes
import numpy as np
from jax import lax
from jax.experimental import pallas as pl
from jax.experimental.pallas import tpu as pltpu
from jax.sharding import PartitionSpec as P

MESH = pl.DeviceIdType.MESH
BF16 = jnp.bfloat16
F32 = jnp.float32

ROWS = 128
CHANNELS = 4096
FILTERS = 256
TAPS = 7
SPAN = 512
HALO = 8
PEERS = 4
CHUNKS = 8
GROUPS = 4
WIDTH = CHANNELS // (PEERS * CHUNKS)
CHUNK = PEERS * WIDTH
GROUP = CHANNELS // GROUPS
HALF = GROUP // 2
NEAR = 8
SHARDS = 16
COLS = CHANNELS // SHARDS
OUT = PEERS * COLS
TAPCOLS = 3 * CHANNELS // SHARDS


def transform_matrices():
    order = np.concatenate([np.arange(0, SPAN, 2), np.arange(1, SPAN, 2)])
    turns = (np.outer(2 * order + 1, np.arange(SPAN)) % (4 * SPAN)) * (2 * np.pi / (4 * SPAN))
    forward = np.concatenate([np.cos(turns), -np.sin(turns)], axis=0)
    high = forward.astype(ml_dtypes.bfloat16)
    low = (forward - high.astype(np.float64)).astype(ml_dtypes.bfloat16)
    scale = np.float64(1.0 / SPAN)
    back_high = (high.astype(np.float64).T * scale).astype(ml_dtypes.bfloat16)
    back_low = (low.astype(np.float64).T * scale).astype(ml_dtypes.bfloat16)
    return high, low, back_high, back_low


def dot(a, b):
    return jnp.dot(a, b, preferred_element_type=F32)


def mixer_kernel(
    feat, taps_in, filt_in, weight, fwd_hi_in, fwd_lo_in, inv_hi_in, inv_lo_in,
    out,
    ext, tail, filt, halo_out, halo_in, halo, taps_all, taps, fwd_hi, fwd_lo, inv_hi, inv_lo, spec, y_hi, y_lo,
    prod, cur, prev, convs, back, gated, wts, acc, outs,
    local_sem, halo_send, halo_recv, wt_send, wt_recv, tap_send, tap_recv, zf_send, zf_recv, yf_sem, zb_send, zb_recv,
    xg_send, xg_recv, xr_send, xr_recv, wz_send, wz_recv, wy_send, wy_recv, wm_sem, wc_send, wc_recv, o_send, o_recv, own_sem,
):
    ctx, fsdp = lax.axis_index("ctx"), lax.axis_index("fsdp")
    y, zl = ctx // 4, ctx % 4
    x, zh, core = fsdp // 4, (fsdp // 2) % 2, fsdp % 2
    slot = zh * 2 + core
    far_slot = (1 - zh) * 2 + core
    here = x * 2 + core

    def device(y_=y, zl_=zl, x_=x, zh_=zh, core_=core):
        return (y_ * 4 + zl_, (x_ * 2 + zh_) * 2 + core_)

    def remote(src, dst, send, recv, to):
        return pltpu.make_async_remote_copy(
            src_ref=src, dst_ref=dst, send_sem=send, recv_sem=recv, device_id=to, device_id_type=MESH
        )

    def ring(k, at):
        return lax.rem(at + k, PEERS)

    def features_load(part, at):
        lanes = pl.ds(part * CHANNELS, CHANNELS)
        return pltpu.make_async_copy(feat.at[:, lanes], ext.at[:, lanes], local_sem.at[at])

    tail_load = pltpu.make_async_copy(feat.at[pl.ds(ROWS - 16, 16)], tail, local_sem.at[9])
    tail_load.start()
    loads = [
        features_load(1, 0),
        features_load(2, 1),
        pltpu.make_async_copy(fwd_hi_in, fwd_hi, local_sem.at[2]),
        pltpu.make_async_copy(fwd_lo_in, fwd_lo, local_sem.at[3]),
        features_load(0, 4),
        pltpu.make_async_copy(inv_hi_in, inv_hi, local_sem.at[5]),
        pltpu.make_async_copy(inv_lo_in, inv_lo, local_sem.at[6]),
        pltpu.make_async_copy(weight, wts.at[slot], local_sem.at[7]),
        pltpu.make_async_copy(filt_in, filt, local_sem.at[10]),
    ]
    for load in loads:
        load.start()

    barrier = pltpu.get_barrier_semaphore()

    def greet(to):
        pl.semaphore_signal(barrier, inc=1, device_id=to, device_id_type=MESH)

    def near(k):
        other = lax.rem(x * 2 + core + k, NEAR)
        return other // 2, lax.rem(other, 2)

    def greet_near(k, carry):
        x_, core_ = near(k)
        greet(device(x_=x_, core_=core_))
        return carry

    lax.fori_loop(1, NEAR, greet_near, 0)
    for k in range(1, PEERS):
        greet(device(zl_=ring(k, zl)))
        greet(device(y_=ring(k, y)))
    after, before = lax.rem(ctx + 1, 16), lax.rem(ctx + 15, 16)
    greet((after, fsdp))
    greet((before, fsdp))
    greet(device(zl_=3 - zl, zh_=1 - zh))
    greet(device(zl_=ring(2, zl), zh_=1 - zh))

    own_taps = jnp.concatenate([taps_in[...].astype(F32), jnp.zeros((8 - TAPS, TAPCOLS), F32)], axis=0)
    own_taps = jnp.concatenate([own_taps[:, : TAPCOLS // 2], own_taps[:, TAPCOLS // 2 :]], axis=0)
    taps_all[here, zh] = own_taps.astype(BF16)

    tail_load.wait()

    def pack(part, group):
        rows = tail[:, part * CHANNELS + group * GROUP : part * CHANNELS + (group + 1) * GROUP].astype(F32)[16 - HALO :]
        packed = jnp.concatenate([rows[:, :HALF], rows[:, HALF:]], axis=0)
        return packed.astype(BF16)

    for group in range(GROUPS):
        halo_out[group, 0] = pack(1, group)
        halo_out[group, 1] = pack(2, group)
        halo_out[GROUPS + group // 2, group % 2] = pack(0, group)

    pl.semaphore_wait(barrier, NEAR - 1 + 2 * (PEERS - 1) + 4)

    def far_taps(j, to_zl):
        ref = taps_all.at[here, zh]
        return remote(ref, ref, wt_send.at[j], wt_recv, device(zl_=to_zl, zh_=1 - zh))

    @pl.when(zl == 0)
    def _():
        far_taps(1, 2).start()
        far_taps(0, 3).start()

    @pl.when(zl == 3)
    def _():
        far_taps(1, 1).start()
        far_taps(0, 0).start()

    def tap_copy(k):
        x_, core_ = near(k)
        return remote(taps_all.at[here], taps_all.at[here], tap_send.at[k], tap_recv.at[here], device(x_=x_, core_=core_))

    def tap_arrival(k):
        x_, core_ = near(k)
        there = x_ * 2 + core_
        return remote(taps_all.at[there], taps_all.at[there], tap_send.at[k], tap_recv.at[there], device(x_=x_, core_=core_))

    def halo_copy(at):
        return remote(halo_out.at[at], halo_in.at[at], halo_send.at[at], halo_recv.at[at], (after, fsdp))

    for group in range(GROUPS):
        halo_copy(group).start()

    ref = taps_all.at[here, 1 - zh]
    remote(ref, ref, wt_send.at[0], wt_recv, device(zl_=3 - zl, zh_=1 - zh)).wait_recv()
    for k in (4, 3, 5, 2, 6, 1, 7):
        tap_copy(k).start()

    def quarter(ref, which):
        return ref.at[pl.ds(pl.multiple_of(which * GROUP, GROUP), GROUP)]

    mate = device(core_=1 - core)
    mate_copy = remote(weight, wts.at[slot], wm_sem.at[0], wm_sem.at[1], mate)

    def far_copy(j, to_zl):
        return remote(quarter(weight, y), quarter(wts.at[slot], y), wz_send.at[j], wz_recv, device(zl_=to_zl, zh_=1 - zh))

    @pl.when(zl == 0)
    def _():
        far_copy(1, 2).start()
        far_copy(0, 3).start()

    @pl.when(zl == 3)
    def _():
        far_copy(1, 1).start()
        far_copy(0, 0).start()

    loads[2].wait()
    loads[3].wait()
    loads[8].wait()
    mine_filt = filt[:, pl.ds(pl.multiple_of(lax.rem(zl, FILTERS // WIDTH) * WIDTH, WIDTH), WIDTH)]
    for part in range(4):
        rows = pl.ds(part * 256, 256)
        spec[rows, :] = dot(fwd_hi[rows, :], mine_filt) + dot(fwd_lo[rows, :], mine_filt)

    @pl.when(y == 0)
    def _():
        prev[...] = jnp.zeros(prev.shape, BF16)

    loads[0].wait()
    loads[1].wait()
    loads[4].wait()

    for k in range(1, NEAR):
        tap_arrival(k).wait_recv()
    for shard in range(SHARDS):
        block = taps_all[shard // 4 * 2 + shard % 2, shard // 2 % 2].astype(F32)
        taps[:, pl.ds(shard * TAPCOLS, TAPCOLS // 2)] = block[:8]
        taps[:, pl.ds(shard * TAPCOLS + TAPCOLS // 2, TAPCOLS // 2)] = block[8:]

    keep = jnp.where(ctx > 0, 1.0, 0.0).astype(F32)

    def unpack(at, which, begin):
        block = halo_in[at, which].astype(F32) * keep
        halo[:, pl.ds(pl.multiple_of(begin, HALF), HALF)] = block[:HALO]
        halo[:, pl.ds(pl.multiple_of(begin + HALF, HALF), HALF)] = block[HALO:]

    def short_filter(begin):
        columns = pl.ds(pl.multiple_of(begin, 128), 128)
        rows = jnp.concatenate([halo[:, columns], ext[:, columns].astype(F32)], axis=0)
        weights = taps[:, columns]
        total = weights[0:1] * rows[HALO:]
        for lag in range(1, TAPS):
            total = total + weights[lag : lag + 1] * pltpu.roll(rows, lag, 0)[HALO:]
        return total

    def own_rows(which):
        return pl.ds(pl.multiple_of(which * ROWS, ROWS), ROWS)

    def zf_copy(i, k):
        q = ring(k, zl)
        return remote(prod.at[i, q], cur.at[i, own_rows(zl)], zf_send.at[i, k], zf_recv.at[i, zl], device(zl_=q))

    def zf_arrival(i, k):
        q = ring(k, zl)
        return remote(prod.at[i, q], cur.at[i, own_rows(q)], zf_send.at[i, k], zf_recv.at[i, q], device(zl_=q))

    def products(i):
        group = i // 2

        @pl.when(lax.rem(i, 2) == 0)
        def _():
            halo_copy(group).wait_recv()
            unpack(group, 0, CHANNELS + group * GROUP)
            unpack(group, 1, 2 * CHANNELS + group * GROUP)

        def one(q, inner):
            begin = i * CHUNK + q * WIDTH
            keys = short_filter(CHANNELS + begin)
            values = short_filter(2 * CHANNELS + begin)
            prod[i, q] = (keys * values).astype(BF16)
            return inner

        lax.fori_loop(0, PEERS, one, 0)
        for k in range(1, PEERS):
            zf_copy(i, k).start()
        cur[i, own_rows(zl), :] = prod[i, zl]

        @pl.when(i == 1)
        def _():
            for at in (GROUPS, GROUPS + 1):
                halo_copy(at).start()


    def yf_copy(i):
        return remote(cur.at[i], prev.at[i], yf_sem.at[0, i], yf_sem.at[1, i], device(y_=ring(1, y)))

    def onward(i):
        for k in range(1, PEERS):
            zf_arrival(i, k).wait_recv()

        @pl.when(y < PEERS - 1)
        def _():
            yf_copy(i).start()

    def zb_copy(i, k):
        q = ring(k, zl)
        return remote(convs.at[i, own_rows(q)], back.at[i, zl], zb_send.at[i, k], zb_recv.at[i, zl], device(zl_=q))

    def zb_arrival(i, k):
        q = ring(k, zl)
        return remote(convs.at[i, own_rows(q)], back.at[i, q], zb_send.at[i, k], zb_recv.at[i, q], device(zl_=q))

    def convolve(i):
        @pl.when(y > 0)
        def _():
            yf_copy(i).wait_recv()

        def frequencies(part, carry):
            real = pl.ds(pl.multiple_of(part * 128, 128), 128)
            imag = pl.ds(pl.multiple_of(SPAN + part * 128, 128), 128)
            both = jnp.concatenate([cur[i], prev[i]], axis=1)
            re = dot(fwd_hi[real, :], both) + dot(fwd_lo[real, :], both)
            im = dot(fwd_hi[imag, :], both) + dot(fwd_lo[imag, :], both)
            sign = jnp.where(part < 2, 1.0, -1.0).astype(F32)
            a = re[:, :WIDTH] - sign * im[:, WIDTH:]
            b = im[:, :WIDTH] + sign * re[:, WIDTH:]
            hr, hi = spec[real, :], spec[imag, :]
            yr = hr * a - hi * b
            yi = hr * b + hi * a
            yr_hi, yi_hi = yr.astype(BF16), yi.astype(BF16)
            y_hi[real, :] = yr_hi
            y_hi[imag, :] = yi_hi
            y_lo[real, :] = (yr - yr_hi.astype(F32)).astype(BF16)
            y_lo[imag, :] = (yi - yi_hi.astype(F32)).astype(BF16)
            return carry

        lax.fori_loop(0, 4, frequencies, 0)

        def positions(part, carry):
            rows = own_rows(part)
            both = dot(inv_hi[rows, :], jnp.concatenate([y_hi[...], y_lo[...]], axis=1))
            got = both[:, :WIDTH] + both[:, WIDTH:] + dot(inv_lo[rows, :], y_hi[...])
            convs[i, rows, :] = got.astype(BF16)
            return carry

        lax.fori_loop(0, PEERS, positions, 0)
        for k in range(1, PEERS):
            zb_copy(i, k).start()
        back[i, zl] = convs[i, own_rows(zl), :]

    left, right = ring(3, x), ring(1, x)

    def half(i, source, at):
        return gated.at[i, source, pl.ds(at * (ROWS // 2), ROWS // 2)]

    def xg_copy(i, to, at, which):
        ref = half(i, x, which)
        return remote(ref, ref, xg_send.at[i, at, which], xg_recv.at[i, at, which], device(x_=to))

    def xg_arrival(i, source, at, which):
        ref = half(i, source, which)
        return remote(ref, ref, xg_send.at[i, at, which], xg_recv.at[i, at, which], device(x_=source))

    def xr_copy(i, source, to, at):
        ref = half(i, source, at)
        return remote(ref, ref, xr_send.at[i, at], xr_recv.at[i, at], device(x_=to))

    def gate(i):
        @pl.when(i == 0)
        def _():
            for at in (GROUPS, GROUPS + 1):
                halo_copy(at).wait_recv()
            for group in range(GROUPS):
                unpack(GROUPS + group // 2, group % 2, group * GROUP)

        for k in range(1, PEERS):
            zb_arrival(i, k).wait_recv()
        for q in range(PEERS):
            query = short_filter(i * CHUNK + q * WIDTH)
            gated[i, x, :, q * WIDTH : (q + 1) * WIDTH] = (query * back[i, q].astype(F32)).astype(BF16)
        xg_copy(i, right, 0, 0).start()
        xg_copy(i, left, 1, 1).start()
        xg_copy(i, right, 0, 1).start()
        xg_copy(i, left, 1, 0).start()

    def relay(i):
        xg_arrival(i, left, 0, 0).wait_recv()
        xr_copy(i, left, right, 0).start()
        xg_arrival(i, right, 1, 1).wait_recv()
        xr_copy(i, right, left, 1).start()

    def far_arrivals(i):
        across = ring(2, x)
        xg_arrival(i, left, 0, 1).wait_recv()
        xg_arrival(i, right, 1, 0).wait_recv()
        xr_copy(i, across, left, 0).wait_recv()
        xr_copy(i, across, right, 1).wait_recv()

    def project(group, zh_):
        lhs = [gated[2 * group + part].reshape(PEERS * ROWS, CHUNK) for part in range(2)]

        def block(c, carry):
            j = zh_ * 2 + c
            term = acc[j]
            for part in range(2):
                term = term + dot(lhs[part], wts[j, pl.ds(pl.multiple_of(group * GROUP + part * CHUNK, CHUNK), CHUNK), :])
            acc[j] = term
            return carry

        lax.fori_loop(0, 2, block, 0)

    def wy_copy(k):
        ref = quarter(wts.at[far_slot], ring(k, y))
        return remote(ref, ref, wy_send.at[k], wy_recv.at[k], device(y_=ring(3, y)))

    def wy_arrival(k):
        ref = quarter(wts.at[far_slot], ring(k + 1, y))
        return remote(ref, ref, wy_send.at[k], wy_recv.at[k], device(y_=ring(1, y)))

    def wc_copy(which):
        ref = quarter(wts.at[far_slot], which)
        return remote(ref, ref, wc_send.at[which], wc_recv.at[which], mate)

    def wc_arrival(which):
        ref = quarter(wts.at[(1 - zh) * 2 + 1 - core], which)
        return remote(ref, ref, wc_send.at[which], wc_recv.at[which], mate)

    def columns_first():
        far = quarter(wts.at[far_slot], y)
        remote(far, far, wz_send.at[0], wz_recv, device(zl_=3 - zl, zh_=1 - zh)).wait_recv()
        wy_copy(0).start()
        wc_copy(y).start()

    def columns_next(k):
        wy_arrival(k - 1).wait_recv()

        @pl.when(k < PEERS - 1)
        def _():
            wy_copy(k).start()

        wc_copy(ring(k, y)).start()

    loads[5].wait()
    loads[6].wait()
    acc[...] = jnp.zeros(acc.shape, F32)

    def step(t, carry):
        @pl.when(t < CHUNKS)
        def _():
            products(t)

        @pl.when(jnp.logical_and(t >= 2, t < CHUNKS + 2))
        def _():
            onward(t - 2)

        @pl.when(jnp.logical_and(t >= 3, t < CHUNKS + 3))
        def _():
            convolve(t - 3)

        @pl.when(jnp.logical_and(t >= 4, t < CHUNKS + 4))
        def _():
            gate(t - 4)

        @pl.when(t >= 5)
        def _():
            relay(t - 5)

        @pl.when(t == 3)
        def _():
            mate_copy.start()

        @pl.when(t == 4)
        def _():
            columns_first()

        @pl.when(jnp.logical_or(t == 6, jnp.logical_or(t == 8, t == 10)))
        def _():
            columns_next((t - 4) // 2)

        @pl.when(t == 9)
        def _():
            loads[7].wait()
            mate_copy.wait_recv()

        @pl.when(t >= 9)
        def _():
            far_arrivals(2 * (t - 9))
            far_arrivals(2 * (t - 9) + 1)
            project(t - 9, zh)

        return carry

    lax.fori_loop(0, CHUNKS + 4, step, 0)

    def out_columns(x_, zh_):
        return out.at[:, pl.ds(pl.multiple_of(x_ * OUT + zh_ * (OUT // 2), OUT // 2), OUT // 2)]

    def out_copy(zh_, k):
        q = ring(k, x)
        return remote(outs.at[zh_, q], out_columns(x, zh_), o_send.at[zh_, k], o_recv.at[zh_, x], device(x_=q))

    def out_arrival(zh_, k):
        q = ring(k, x)
        return remote(outs.at[zh_, q], out_columns(q, zh_), o_send.at[zh_, k], o_recv.at[zh_, q], device(x_=q))

    def out_own(zh_):
        return pltpu.make_async_copy(outs.at[zh_, x], out_columns(x, zh_), own_sem.at[zh_])

    last = GROUPS - 1

    def finish(zh_):
        def one(k, carry):
            q = ring(k, x)
            lhs = jnp.concatenate([gated[2 * last, q], gated[2 * last + 1, q]], axis=1)
            for c in range(2):
                j = zh_ * 2 + c
                total = acc[j, own_rows(q), :] + dot(lhs, wts[j, last * GROUP :, :])
                outs[zh_, q, :, c * COLS : (c + 1) * COLS] = total.astype(BF16)

            @pl.when(k < PEERS)
            def _():
                out_copy(zh_, k).start()

            return carry

        lax.fori_loop(1, PEERS + 1, one, 0)
        out_own(zh_).start()

    relay(CHUNKS - 1)

    def arrived(which, carry):
        wc_arrival(which).wait_recv()
        return carry

    lax.fori_loop(0, PEERS, arrived, 0)

    def project_far(group, carry):
        project(group, 1 - zh)
        return carry

    lax.fori_loop(0, last, project_far, 0)
    for i in range(2 * last, CHUNKS):
        far_arrivals(i)
    finish(zh)
    finish(1 - zh)
    for zh_ in range(2):
        out_own(zh_).wait()
        for k in range(1, PEERS):
            out_arrival(zh_, k).wait_recv()

    mate_copy.wait_send()
    for at in range(GROUPS + 2):
        halo_copy(at).wait_send()

    for k in range(1, NEAR):
        tap_copy(k).wait_send()

    @pl.when(jnp.logical_or(zl == 0, zl == 3))
    def _():
        far_copy(0, 3 - zl).wait_send()
        far_copy(1, ring(2, zl)).wait_send()
        far_taps(0, 3 - zl).wait_send()
        far_taps(1, ring(2, zl)).wait_send()

    for k in range(1, PEERS):
        wy_copy(k - 1).wait_send()
        out_copy(0, k).wait_send()
        out_copy(1, k).wait_send()
    for which in range(PEERS):
        wc_copy(which).wait_send()

    def sent_chunk(i, carry):
        for k in range(1, PEERS):
            zf_copy(i, k).wait_send()
            zb_copy(i, k).wait_send()
        for which in range(2):
            xg_copy(i, right, 0, which).wait_send()
            xg_copy(i, left, 1, which).wait_send()
        xr_copy(i, left, right, 0).wait_send()
        xr_copy(i, right, left, 1).wait_send()

        @pl.when(y < PEERS - 1)
        def _():
            yf_copy(i).wait_send()

        return carry

    lax.fori_loop(0, CHUNKS, sent_chunk, 0)


def shards(features, short_weight, long_filter, out_weight):
    matrices = [jnp.asarray(m) for m in transform_matrices()]
    anywhere = pl.BlockSpec(memory_space=pl.ANY)
    dma = pltpu.SemaphoreType.DMA
    result = pl.pallas_call(
        mixer_kernel,
        name="mixer",
        out_shape=jax.ShapeDtypeStruct((ROWS, CHANNELS), BF16),
        in_specs=[anywhere, pl.BlockSpec(memory_space=pltpu.VMEM)] + [anywhere] * 6,
        out_specs=anywhere,
        scratch_shapes=[
            pltpu.VMEM((ROWS, 3 * CHANNELS), BF16),
            pltpu.VMEM((16, 3 * CHANNELS), BF16),
            pltpu.VMEM((SPAN, FILTERS), BF16),
            pltpu.VMEM((GROUPS + 2, 2, 2 * HALO, HALF), BF16),
            pltpu.VMEM((GROUPS + 2, 2, 2 * HALO, HALF), BF16),
            pltpu.VMEM((HALO, 3 * CHANNELS), F32),
            pltpu.VMEM((NEAR, 2, 16, TAPCOLS // 2), BF16),
            pltpu.VMEM((8, 3 * CHANNELS), F32),
            pltpu.VMEM((2 * SPAN, SPAN), BF16),
            pltpu.VMEM((2 * SPAN, SPAN), BF16),
            pltpu.VMEM((SPAN, 2 * SPAN), BF16),
            pltpu.VMEM((SPAN, 2 * SPAN), BF16),
            pltpu.VMEM((2 * SPAN, WIDTH), F32),
            pltpu.VMEM((2 * SPAN, WIDTH), BF16),
            pltpu.VMEM((2 * SPAN, WIDTH), BF16),
            pltpu.VMEM((CHUNKS, PEERS, ROWS, WIDTH), BF16),
            pltpu.VMEM((CHUNKS, SPAN, WIDTH), BF16),
            pltpu.VMEM((CHUNKS, SPAN, WIDTH), BF16),
            pltpu.VMEM((CHUNKS, SPAN, WIDTH), BF16),
            pltpu.VMEM((CHUNKS, PEERS, ROWS, WIDTH), BF16),
            pltpu.VMEM((CHUNKS, PEERS, ROWS, CHUNK), BF16),
            pltpu.VMEM((PEERS, CHANNELS, COLS), BF16),
            pltpu.VMEM((PEERS, PEERS * ROWS, COLS), F32),
            pltpu.VMEM((2, PEERS, ROWS, OUT // 2), BF16),
            dma((11,)), dma((GROUPS + 2,)), dma((GROUPS + 2,)), dma((2,)), dma, dma((NEAR,)), dma((NEAR,)),
            dma((CHUNKS, PEERS)), dma((CHUNKS, PEERS)), dma((2, CHUNKS)), dma((CHUNKS, PEERS)), dma((CHUNKS, PEERS)),
            dma((CHUNKS, 2, 2)), dma((CHUNKS, 2, 2)), dma((CHUNKS, 2)), dma((CHUNKS, 2)),
            dma((2,)), dma, dma((PEERS,)), dma((PEERS,)), dma((2,)), dma((PEERS,)), dma((PEERS,)), dma((2, PEERS)), dma((2, PEERS)), dma((2,)),
        ],
        compiler_params=pltpu.CompilerParams(collective_id=0, has_side_effects=True, vmem_limit_bytes=56 * 2**20),
    )(features[0], short_weight, long_filter, out_weight, *matrices)
    return result[None]


def solution(mesh):
    placed = (P("fsdp", "ctx", None), P(None, "fsdp"), P(), P(None, "fsdp"))
    return jax.shard_map(
        shards, mesh=mesh, in_specs=placed, out_specs=P("fsdp", "ctx", None), check_vma=False
    )
```

```python
import functools

import jax
import jax.numpy as jnp
import ml_dtypes
import numpy as np
from jax import lax
from jax.experimental import pallas as pl
from jax.experimental.pallas import tpu as pltpu
from jax.sharding import PartitionSpec as P

MESH = pl.DeviceIdType.MESH
BF16 = jnp.bfloat16
F32 = jnp.float32

ROWS = 128
CHANNELS = 4096
FILTERS = 256
TAPS = 7
SPAN = 512
HALO = 8
PEERS = 4
CHUNKS = 8
GROUPS = 4
WIDTH = CHANNELS // (PEERS * CHUNKS)
CHUNK = PEERS * WIDTH
GROUP = CHANNELS // GROUPS
HALF = GROUP // 2
NEAR = 8
SHARDS = 16
COLS = CHANNELS // SHARDS
OUT = PEERS * COLS
TAPCOLS = 3 * CHANNELS // SHARDS


def transform_matrices():
    order = np.concatenate([np.arange(0, SPAN, 2), np.arange(1, SPAN, 2)])
    turns = (np.outer(2 * order + 1, np.arange(SPAN)) % (4 * SPAN)) * (2 * np.pi / (4 * SPAN))
    forward = np.concatenate([np.cos(turns), -np.sin(turns)], axis=0)
    high = forward.astype(ml_dtypes.bfloat16)
    low = (forward - high.astype(np.float64)).astype(ml_dtypes.bfloat16)
    scale = np.float64(1.0 / SPAN)
    back_high = (high.astype(np.float64).T * scale).astype(ml_dtypes.bfloat16)
    back_low = (low.astype(np.float64).T * scale).astype(ml_dtypes.bfloat16)
    return high, low, back_high, back_low


def dot(a, b):
    return jnp.dot(a, b, preferred_element_type=F32)


def mixer_kernel(
    feat, taps_in, filt_in, weight, fwd_hi_in, fwd_lo_in, inv_hi_in, inv_lo_in,
    out,
    ext, tail, filt, halo_out, halo_in, halo, taps_all, taps, fwd_hi, fwd_lo, inv_hi, inv_lo, spec, y_hi, y_lo,
    prod, cur, prev, convs, back, gated, wts, acc, outs,
    local_sem, halo_send, halo_recv, wt_send, wt_recv, tap_send, tap_recv, zf_send, zf_recv, yf_sem, zb_send, zb_recv,
    xg_send, xg_recv, xr_send, xr_recv, wz_send, wz_recv, wy_send, wy_recv, wm_sem, wc_send, wc_recv, o_send, o_recv, own_sem,
):
    ctx, fsdp = lax.axis_index("ctx"), lax.axis_index("fsdp")
    y, zl = ctx // 4, ctx % 4
    x, zh, core = fsdp // 4, (fsdp // 2) % 2, fsdp % 2
    slot = zh * 2 + core
    far_slot = (1 - zh) * 2 + core
    here = x * 2 + core

    def device(y_=y, zl_=zl, x_=x, zh_=zh, core_=core):
        return (y_ * 4 + zl_, (x_ * 2 + zh_) * 2 + core_)

    def remote(src, dst, send, recv, to):
        return pltpu.make_async_remote_copy(
            src_ref=src, dst_ref=dst, send_sem=send, recv_sem=recv, device_id=to, device_id_type=MESH
        )

    def ring(k, at):
        return lax.rem(at + k, PEERS)

    def features_load(part, at):
        lanes = pl.ds(part * CHANNELS, CHANNELS)
        return pltpu.make_async_copy(feat.at[:, lanes], ext.at[:, lanes], local_sem.at[at])

    tail_load = pltpu.make_async_copy(feat.at[pl.ds(ROWS - 16, 16)], tail, local_sem.at[9])
    tail_load.start()
    loads = [
        features_load(1, 0),
        features_load(2, 1),
        pltpu.make_async_copy(fwd_hi_in, fwd_hi, local_sem.at[2]),
        pltpu.make_async_copy(fwd_lo_in, fwd_lo, local_sem.at[3]),
        features_load(0, 4),
        pltpu.make_async_copy(inv_hi_in, inv_hi, local_sem.at[5]),
        pltpu.make_async_copy(inv_lo_in, inv_lo, local_sem.at[6]),
        pltpu.make_async_copy(weight, wts.at[slot], local_sem.at[7]),
        pltpu.make_async_copy(filt_in, filt, local_sem.at[10]),
    ]
    for load in loads:
        load.start()

    barrier = pltpu.get_barrier_semaphore()

    def greet(to):
        pl.semaphore_signal(barrier, inc=1, device_id=to, device_id_type=MESH)

    def near(k):
        other = lax.rem(x * 2 + core + k, NEAR)
        return other // 2, lax.rem(other, 2)

    def greet_near(k, carry):
        x_, core_ = near(k)
        greet(device(x_=x_, core_=core_))
        return carry

    lax.fori_loop(1, NEAR, greet_near, 0)
    for k in range(1, PEERS):
        greet(device(zl_=ring(k, zl)))
        greet(device(y_=ring(k, y)))
    after, before = lax.rem(ctx + 1, 16), lax.rem(ctx + 15, 16)
    greet((after, fsdp))
    greet((before, fsdp))
    greet(device(zl_=3 - zl, zh_=1 - zh))
    greet(device(zl_=ring(2, zl), zh_=1 - zh))

    own_taps = jnp.concatenate([taps_in[...].astype(F32), jnp.zeros((8 - TAPS, TAPCOLS), F32)], axis=0)
    own_taps = jnp.concatenate([own_taps[:, : TAPCOLS // 2], own_taps[:, TAPCOLS // 2 :]], axis=0)
    taps_all[here, zh] = own_taps.astype(BF16)

    tail_load.wait()

    def pack(part, group):
        rows = tail[:, part * CHANNELS + group * GROUP : part * CHANNELS + (group + 1) * GROUP].astype(F32)[16 - HALO :]
        packed = jnp.concatenate([rows[:, :HALF], rows[:, HALF:]], axis=0)
        return packed.astype(BF16)

    for group in range(GROUPS):
        halo_out[group, 0] = pack(1, group)
        halo_out[group, 1] = pack(2, group)
        halo_out[GROUPS + group // 2, group % 2] = pack(0, group)

    pl.semaphore_wait(barrier, NEAR - 1 + 2 * (PEERS - 1) + 4)

    def far_taps(j, to_zl):
        ref = taps_all.at[here, zh]
        return remote(ref, ref, wt_send.at[j], wt_recv, device(zl_=to_zl, zh_=1 - zh))

    @pl.when(zl == 0)
    def _():
        far_taps(1, 2).start()
        far_taps(0, 3).start()

    @pl.when(zl == 3)
    def _():
        far_taps(1, 1).start()
        far_taps(0, 0).start()

    def tap_copy(k):
        x_, core_ = near(k)
        return remote(taps_all.at[here], taps_all.at[here], tap_send.at[k], tap_recv.at[here], device(x_=x_, core_=core_))

    def tap_arrival(k):
        x_, core_ = near(k)
        there = x_ * 2 + core_
        return remote(taps_all.at[there], taps_all.at[there], tap_send.at[k], tap_recv.at[there], device(x_=x_, core_=core_))

    def halo_copy(at):
        return remote(halo_out.at[at], halo_in.at[at], halo_send.at[at], halo_recv.at[at], (after, fsdp))

    for group in range(GROUPS):
        halo_copy(group).start()

    ref = taps_all.at[here, 1 - zh]
    remote(ref, ref, wt_send.at[0], wt_recv, device(zl_=3 - zl, zh_=1 - zh)).wait_recv()
    for k in (4, 3, 5, 2, 6, 1, 7):
        tap_copy(k).start()

    def quarter(ref, which):
        return ref.at[pl.ds(pl.multiple_of(which * GROUP, GROUP), GROUP)]

    mate = device(core_=1 - core)
    mate_copy = remote(weight, wts.at[slot], wm_sem.at[0], wm_sem.at[1], mate)

    def far_copy(j, to_zl):
        return remote(quarter(weight, y), quarter(wts.at[slot], y), wz_send.at[j], wz_recv, device(zl_=to_zl, zh_=1 - zh))

    @pl.when(zl == 0)
    def _():
        far_copy(1, 2).start()
        far_copy(0, 3).start()

    @pl.when(zl == 3)
    def _():
        far_copy(1, 1).start()
        far_copy(0, 0).start()

    loads[2].wait()
    loads[3].wait()
    loads[8].wait()
    mine_filt = filt[:, pl.ds(pl.multiple_of(lax.rem(zl, FILTERS // WIDTH) * WIDTH, WIDTH), WIDTH)]
    for part in range(4):
        rows = pl.ds(part * 256, 256)
        spec[rows, :] = dot(fwd_hi[rows, :], mine_filt) + dot(fwd_lo[rows, :], mine_filt)

    @pl.when(y == 0)
    def _():
        prev[...] = jnp.zeros(prev.shape, BF16)

    loads[0].wait()
    loads[1].wait()
    loads[4].wait()

    for k in range(1, NEAR):
        tap_arrival(k).wait_recv()
    for shard in range(SHARDS):
        block = taps_all[shard // 4 * 2 + shard % 2, shard // 2 % 2].astype(F32)
        taps[:, pl.ds(shard * TAPCOLS, TAPCOLS // 2)] = block[:8]
        taps[:, pl.ds(shard * TAPCOLS + TAPCOLS // 2, TAPCOLS // 2)] = block[8:]

    keep = jnp.where(ctx > 0, 1.0, 0.0).astype(F32)

    def unpack(at, which, begin):
        block = halo_in[at, which].astype(F32) * keep
        halo[:, pl.ds(pl.multiple_of(begin, HALF), HALF)] = block[:HALO]
        halo[:, pl.ds(pl.multiple_of(begin + HALF, HALF), HALF)] = block[HALO:]

    def short_filter(begin):
        columns = pl.ds(pl.multiple_of(begin, 128), 128)
        rows = jnp.concatenate([halo[:, columns], ext[:, columns].astype(F32)], axis=0)
        weights = taps[:, columns]
        total = weights[0:1] * rows[HALO:]
        for lag in range(1, TAPS):
            total = total + weights[lag : lag + 1] * pltpu.roll(rows, lag, 0)[HALO:]
        return total

    def own_rows(which):
        return pl.ds(pl.multiple_of(which * ROWS, ROWS), ROWS)

    def across_first(k):
        return (lax.rem(zl + 2, PEERS), 3 - zl, zl + 1 - 2 * lax.rem(zl, 2))[k - 1]

    def zf_copy(i, k):
        q = across_first(k)
        return remote(prod.at[i, q], cur.at[i, own_rows(zl)], zf_send.at[i, k], zf_recv.at[i, zl], device(zl_=q))

    def zf_arrival(i, k):
        q = across_first(k)
        return remote(prod.at[i, q], cur.at[i, own_rows(q)], zf_send.at[i, k], zf_recv.at[i, q], device(zl_=q))

    def products(i):
        group = i // 2

        @pl.when(lax.rem(i, 2) == 0)
        def _():
            halo_copy(group).wait_recv()
            unpack(group, 0, CHANNELS + group * GROUP)
            unpack(group, 1, 2 * CHANNELS + group * GROUP)

        def one(q):
            begin = i * CHUNK + q * WIDTH
            keys = short_filter(CHANNELS + begin)
            values = short_filter(2 * CHANNELS + begin)
            return (keys * values).astype(BF16)

        for k in range(1, PEERS):
            prod[i, across_first(k)] = one(across_first(k))
            zf_copy(i, k).start()
        cur[i, own_rows(zl), :] = one(zl)

        @pl.when(i == 1)
        def _():
            for at in (GROUPS, GROUPS + 1):
                halo_copy(at).start()


    def yf_copy(i):
        return remote(cur.at[i], prev.at[i], yf_sem.at[0, i], yf_sem.at[1, i], device(y_=ring(1, y)))

    def onward(i):
        for k in range(1, PEERS):
            zf_arrival(i, k).wait_recv()

        @pl.when(y < PEERS - 1)
        def _():
            yf_copy(i).start()

    def zb_copy(i, k):
        q = across_first(k)
        return remote(convs.at[i, own_rows(q)], back.at[i, zl], zb_send.at[i, k], zb_recv.at[i, zl], device(zl_=q))

    def zb_arrival(i, k):
        q = across_first(k)
        return remote(convs.at[i, own_rows(q)], back.at[i, q], zb_send.at[i, k], zb_recv.at[i, q], device(zl_=q))

    def convolve(i):
        @pl.when(y > 0)
        def _():
            yf_copy(i).wait_recv()

        def frequencies(part, carry):
            real = pl.ds(pl.multiple_of(part * 128, 128), 128)
            imag = pl.ds(pl.multiple_of(SPAN + part * 128, 128), 128)
            both = jnp.concatenate([cur[i], prev[i]], axis=1)
            re = dot(fwd_hi[real, :], both) + dot(fwd_lo[real, :], both)
            im = dot(fwd_hi[imag, :], both) + dot(fwd_lo[imag, :], both)
            sign = jnp.where(part < 2, 1.0, -1.0).astype(F32)
            a = re[:, :WIDTH] - sign * im[:, WIDTH:]
            b = im[:, :WIDTH] + sign * re[:, WIDTH:]
            hr, hi = spec[real, :], spec[imag, :]
            yr = hr * a - hi * b
            yi = hr * b + hi * a
            yr_hi, yi_hi = yr.astype(BF16), yi.astype(BF16)
            y_hi[real, :] = yr_hi
            y_hi[imag, :] = yi_hi
            y_lo[real, :] = (yr - yr_hi.astype(F32)).astype(BF16)
            y_lo[imag, :] = (yi - yi_hi.astype(F32)).astype(BF16)
            return carry

        lax.fori_loop(0, 4, frequencies, 0)

        def positions(part):
            rows = own_rows(part)
            both = dot(inv_hi[rows, :], jnp.concatenate([y_hi[...], y_lo[...]], axis=1))
            got = both[:, :WIDTH] + both[:, WIDTH:] + dot(inv_lo[rows, :], y_hi[...])
            return got.astype(BF16)

        for k in range(1, PEERS):
            convs[i, own_rows(across_first(k)), :] = positions(across_first(k))
            zb_copy(i, k).start()
        back[i, zl] = positions(zl)

    left, right = ring(3, x), ring(1, x)

    def half(i, source, at):
        return gated.at[i, source, pl.ds(at * (ROWS // 2), ROWS // 2)]

    def xg_copy(i, to, at, which):
        ref = half(i, x, which)
        return remote(ref, ref, xg_send.at[i, at, which], xg_recv.at[i, at, which], device(x_=to))

    def xg_arrival(i, source, at, which):
        ref = half(i, source, which)
        return remote(ref, ref, xg_send.at[i, at, which], xg_recv.at[i, at, which], device(x_=source))

    def xr_copy(i, source, to, at):
        ref = half(i, source, at)
        return remote(ref, ref, xr_send.at[i, at], xr_recv.at[i, at], device(x_=to))

    def gate(i):
        @pl.when(i == 0)
        def _():
            for at in (GROUPS, GROUPS + 1):
                halo_copy(at).wait_recv()
            for group in range(GROUPS):
                unpack(GROUPS + group // 2, group % 2, group * GROUP)

        for k in range(1, PEERS):
            zb_arrival(i, k).wait_recv()
        for q in range(PEERS):
            query = short_filter(i * CHUNK + q * WIDTH)
            gated[i, x, :, q * WIDTH : (q + 1) * WIDTH] = (query * back[i, q].astype(F32)).astype(BF16)
        xg_copy(i, right, 0, 0).start()
        xg_copy(i, left, 1, 1).start()
        xg_copy(i, right, 0, 1).start()
        xg_copy(i, left, 1, 0).start()

    def relay(i):
        xg_arrival(i, left, 0, 0).wait_recv()
        xr_copy(i, left, right, 0).start()
        xg_arrival(i, right, 1, 1).wait_recv()
        xr_copy(i, right, left, 1).start()

    def far_arrivals(i):
        across = ring(2, x)
        xg_arrival(i, left, 0, 1).wait_recv()
        xg_arrival(i, right, 1, 0).wait_recv()
        xr_copy(i, across, left, 0).wait_recv()
        xr_copy(i, across, right, 1).wait_recv()

    def project(group, zh_):
        lhs = [gated[2 * group + part].reshape(PEERS * ROWS, CHUNK) for part in range(2)]

        def block(c, carry):
            j = zh_ * 2 + c
            term = acc[j]
            for part in range(2):
                term = term + dot(lhs[part], wts[j, pl.ds(pl.multiple_of(group * GROUP + part * CHUNK, CHUNK), CHUNK), :])
            acc[j] = term
            return carry

        lax.fori_loop(0, 2, block, 0)

    def wy_copy(k):
        ref = quarter(wts.at[far_slot], ring(k, y))
        return remote(ref, ref, wy_send.at[k], wy_recv.at[k], device(y_=ring(3, y)))

    def wy_arrival(k):
        ref = quarter(wts.at[far_slot], ring(k + 1, y))
        return remote(ref, ref, wy_send.at[k], wy_recv.at[k], device(y_=ring(1, y)))

    def wc_copy(which):
        ref = quarter(wts.at[far_slot], which)
        return remote(ref, ref, wc_send.at[which], wc_recv.at[which], mate)

    def wc_arrival(which):
        ref = quarter(wts.at[(1 - zh) * 2 + 1 - core], which)
        return remote(ref, ref, wc_send.at[which], wc_recv.at[which], mate)

    def columns_first():
        far = quarter(wts.at[far_slot], y)
        remote(far, far, wz_send.at[0], wz_recv, device(zl_=3 - zl, zh_=1 - zh)).wait_recv()
        wy_copy(0).start()
        wc_copy(y).start()

    def columns_next(k):
        wy_arrival(k - 1).wait_recv()

        @pl.when(k < PEERS - 1)
        def _():
            wy_copy(k).start()

        wc_copy(ring(k, y)).start()

    loads[5].wait()
    loads[6].wait()
    acc[...] = jnp.zeros(acc.shape, F32)

    def step(t, carry):
        @pl.when(t < CHUNKS)
        def _():
            products(t)

        @pl.when(jnp.logical_and(t >= 2, t < CHUNKS + 2))
        def _():
            onward(t - 2)

        @pl.when(jnp.logical_and(t >= 3, t < CHUNKS + 3))
        def _():
            convolve(t - 3)

        @pl.when(jnp.logical_and(t >= 4, t < CHUNKS + 4))
        def _():
            gate(t - 4)

        @pl.when(t >= 5)
        def _():
            relay(t - 5)

        @pl.when(t == 3)
        def _():
            mate_copy.start()

        @pl.when(t == 4)
        def _():
            columns_first()

        @pl.when(jnp.logical_or(t == 6, jnp.logical_or(t == 8, t == 10)))
        def _():
            columns_next((t - 4) // 2)

        @pl.when(t == 9)
        def _():
            loads[7].wait()
            mate_copy.wait_recv()

        @pl.when(t >= 9)
        def _():
            far_arrivals(2 * (t - 9))
            far_arrivals(2 * (t - 9) + 1)
            project(t - 9, zh)

        return carry

    lax.fori_loop(0, CHUNKS + 4, step, 0)

    def out_columns(x_, zh_):
        return out.at[:, pl.ds(pl.multiple_of(x_ * OUT + zh_ * (OUT // 2), OUT // 2), OUT // 2)]

    def out_copy(zh_, k):
        q = ring(k, x)
        return remote(outs.at[zh_, q], out_columns(x, zh_), o_send.at[zh_, k], o_recv.at[zh_, x], device(x_=q))

    def out_arrival(zh_, k):
        q = ring(k, x)
        return remote(outs.at[zh_, q], out_columns(q, zh_), o_send.at[zh_, k], o_recv.at[zh_, q], device(x_=q))

    def out_own(zh_):
        return pltpu.make_async_copy(outs.at[zh_, x], out_columns(x, zh_), own_sem.at[zh_])

    last = GROUPS - 1

    def finish(zh_):
        def one(k, carry):
            q = ring(k, x)
            lhs = jnp.concatenate([gated[2 * last, q], gated[2 * last + 1, q]], axis=1)
            for c in range(2):
                j = zh_ * 2 + c
                total = acc[j, own_rows(q), :] + dot(lhs, wts[j, last * GROUP :, :])
                outs[zh_, q, :, c * COLS : (c + 1) * COLS] = total.astype(BF16)

            @pl.when(k < PEERS)
            def _():
                out_copy(zh_, k).start()

            return carry

        lax.fori_loop(1, PEERS + 1, one, 0)
        out_own(zh_).start()

    relay(CHUNKS - 1)

    def arrived(which, carry):
        wc_arrival(which).wait_recv()
        return carry

    lax.fori_loop(0, PEERS, arrived, 0)

    def project_far(group, carry):
        project(group, 1 - zh)
        return carry

    lax.fori_loop(0, last, project_far, 0)
    for i in range(2 * last, CHUNKS):
        far_arrivals(i)
    finish(zh)
    finish(1 - zh)
    for zh_ in range(2):
        out_own(zh_).wait()
        for k in range(1, PEERS):
            out_arrival(zh_, k).wait_recv()

    mate_copy.wait_send()
    for at in range(GROUPS + 2):
        halo_copy(at).wait_send()

    for k in range(1, NEAR):
        tap_copy(k).wait_send()

    @pl.when(jnp.logical_or(zl == 0, zl == 3))
    def _():
        far_copy(0, 3 - zl).wait_send()
        far_copy(1, ring(2, zl)).wait_send()
        far_taps(0, 3 - zl).wait_send()
        far_taps(1, ring(2, zl)).wait_send()

    for k in range(1, PEERS):
        wy_copy(k - 1).wait_send()
        out_copy(0, k).wait_send()
        out_copy(1, k).wait_send()
    for which in range(PEERS):
        wc_copy(which).wait_send()

    def sent_chunk(i, carry):
        for k in range(1, PEERS):
            zf_copy(i, k).wait_send()
            zb_copy(i, k).wait_send()
        for which in range(2):
            xg_copy(i, right, 0, which).wait_send()
            xg_copy(i, left, 1, which).wait_send()
        xr_copy(i, left, right, 0).wait_send()
        xr_copy(i, right, left, 1).wait_send()

        @pl.when(y < PEERS - 1)
        def _():
            yf_copy(i).wait_send()

        return carry

    lax.fori_loop(0, CHUNKS, sent_chunk, 0)


def shards(features, short_weight, long_filter, out_weight):
    matrices = [jnp.asarray(m) for m in transform_matrices()]
    anywhere = pl.BlockSpec(memory_space=pl.ANY)
    dma = pltpu.SemaphoreType.DMA
    result = pl.pallas_call(
        mixer_kernel,
        name="mixer",
        out_shape=jax.ShapeDtypeStruct((ROWS, CHANNELS), BF16),
        in_specs=[anywhere, pl.BlockSpec(memory_space=pltpu.VMEM)] + [anywhere] * 6,
        out_specs=anywhere,
        scratch_shapes=[
            pltpu.VMEM((ROWS, 3 * CHANNELS), BF16),
            pltpu.VMEM((16, 3 * CHANNELS), BF16),
            pltpu.VMEM((SPAN, FILTERS), BF16),
            pltpu.VMEM((GROUPS + 2, 2, 2 * HALO, HALF), BF16),
            pltpu.VMEM((GROUPS + 2, 2, 2 * HALO, HALF), BF16),
            pltpu.VMEM((HALO, 3 * CHANNELS), F32),
            pltpu.VMEM((NEAR, 2, 16, TAPCOLS // 2), BF16),
            pltpu.VMEM((8, 3 * CHANNELS), F32),
            pltpu.VMEM((2 * SPAN, SPAN), BF16),
            pltpu.VMEM((2 * SPAN, SPAN), BF16),
            pltpu.VMEM((SPAN, 2 * SPAN), BF16),
            pltpu.VMEM((SPAN, 2 * SPAN), BF16),
            pltpu.VMEM((2 * SPAN, WIDTH), F32),
            pltpu.VMEM((2 * SPAN, WIDTH), BF16),
            pltpu.VMEM((2 * SPAN, WIDTH), BF16),
            pltpu.VMEM((CHUNKS, PEERS, ROWS, WIDTH), BF16),
            pltpu.VMEM((CHUNKS, SPAN, WIDTH), BF16),
            pltpu.VMEM((CHUNKS, SPAN, WIDTH), BF16),
            pltpu.VMEM((CHUNKS, SPAN, WIDTH), BF16),
            pltpu.VMEM((CHUNKS, PEERS, ROWS, WIDTH), BF16),
            pltpu.VMEM((CHUNKS, PEERS, ROWS, CHUNK), BF16),
            pltpu.VMEM((PEERS, CHANNELS, COLS), BF16),
            pltpu.VMEM((PEERS, PEERS * ROWS, COLS), F32),
            pltpu.VMEM((2, PEERS, ROWS, OUT // 2), BF16),
            dma((11,)), dma((GROUPS + 2,)), dma((GROUPS + 2,)), dma((2,)), dma, dma((NEAR,)), dma((NEAR,)),
            dma((CHUNKS, PEERS)), dma((CHUNKS, PEERS)), dma((2, CHUNKS)), dma((CHUNKS, PEERS)), dma((CHUNKS, PEERS)),
            dma((CHUNKS, 2, 2)), dma((CHUNKS, 2, 2)), dma((CHUNKS, 2)), dma((CHUNKS, 2)),
            dma((2,)), dma, dma((PEERS,)), dma((PEERS,)), dma((2,)), dma((PEERS,)), dma((PEERS,)), dma((2, PEERS)), dma((2, PEERS)), dma((2,)),
        ],
        compiler_params=pltpu.CompilerParams(collective_id=0, has_side_effects=True, vmem_limit_bytes=56 * 2**20),
    )(features[0], short_weight, long_filter, out_weight, *matrices)
    return result[None]


def solution(mesh):
    placed = (P("fsdp", "ctx", None), P(None, "fsdp"), P(), P(None, "fsdp"))
    return jax.shard_map(
        shards, mesh=mesh, in_specs=placed, out_specs=P("fsdp", "ctx", None), check_vma=False
    )
```

```python
import functools

import jax
import jax.numpy as jnp
import ml_dtypes
import numpy as np
from jax import lax
from jax.experimental import pallas as pl
from jax.experimental.pallas import tpu as pltpu
from jax.sharding import PartitionSpec as P

MESH = pl.DeviceIdType.MESH
BF16 = jnp.bfloat16
F32 = jnp.float32

ROWS = 128
CHANNELS = 4096
FILTERS = 256
TAPS = 7
SPAN = 512
HALO = 8
PEERS = 4
CHUNKS = 8
GROUPS = 4
WIDTH = CHANNELS // (PEERS * CHUNKS)
CHUNK = PEERS * WIDTH
GROUP = CHANNELS // GROUPS
HALF = GROUP // 2
NEAR = 8
SHARDS = 16
COLS = CHANNELS // SHARDS
OUT = PEERS * COLS
TAPCOLS = 3 * CHANNELS // SHARDS


def transform_matrices():
    order = np.concatenate([np.arange(0, SPAN, 2), np.arange(1, SPAN, 2)])
    turns = (np.outer(2 * order + 1, np.arange(SPAN)) % (4 * SPAN)) * (2 * np.pi / (4 * SPAN))
    forward = np.concatenate([np.cos(turns), -np.sin(turns)], axis=0)
    high = forward.astype(ml_dtypes.bfloat16)
    low = (forward - high.astype(np.float64)).astype(ml_dtypes.bfloat16)
    scale = np.float64(1.0 / SPAN)
    back_high = (high.astype(np.float64).T * scale).astype(ml_dtypes.bfloat16)
    back_low = (low.astype(np.float64).T * scale).astype(ml_dtypes.bfloat16)
    return high, low, back_high, back_low


def dot(a, b):
    return jnp.dot(a, b, preferred_element_type=F32)


def mixer_kernel(
    feat, taps_in, filt_in, weight, fwd_hi_in, fwd_lo_in, inv_hi_in, inv_lo_in,
    out,
    ext, tail, filt, halo_out, halo_in, halo, taps_all, taps, fwd_hi, fwd_lo, inv_hi, inv_lo, spec, y_hi, y_lo,
    prod, cur, prev, convs, back, gated, wts, acc, outs,
    local_sem, halo_send, halo_recv, wt_send, wt_recv, tap_send, tap_recv, zf_send, zf_recv, yf_sem, zb_send, zb_recv,
    xg_send, xg_recv, xr_send, xr_recv, wz_send, wz_recv, wy_send, wy_recv, wm_sem, wc_send, wc_recv, o_send, o_recv, own_sem,
):
    ctx, fsdp = lax.axis_index("ctx"), lax.axis_index("fsdp")
    y, zl = ctx // 4, ctx % 4
    x, zh, core = fsdp // 4, (fsdp // 2) % 2, fsdp % 2
    slot = zh * 2 + core
    far_slot = (1 - zh) * 2 + core
    here = x * 2 + core

    def device(y_=y, zl_=zl, x_=x, zh_=zh, core_=core):
        return (y_ * 4 + zl_, (x_ * 2 + zh_) * 2 + core_)

    def remote(src, dst, send, recv, to):
        return pltpu.make_async_remote_copy(
            src_ref=src, dst_ref=dst, send_sem=send, recv_sem=recv, device_id=to, device_id_type=MESH
        )

    def ring(k, at):
        return lax.rem(at + k, PEERS)

    def features_load(part, at):
        lanes = pl.ds(part * CHANNELS, CHANNELS)
        return pltpu.make_async_copy(feat.at[:, lanes], ext.at[:, lanes], local_sem.at[at])

    tail_load = pltpu.make_async_copy(feat.at[pl.ds(ROWS - 16, 16)], tail, local_sem.at[9])
    tail_load.start()
    loads = [
        features_load(1, 0),
        features_load(2, 1),
        pltpu.make_async_copy(fwd_hi_in, fwd_hi, local_sem.at[2]),
        pltpu.make_async_copy(fwd_lo_in, fwd_lo, local_sem.at[3]),
        features_load(0, 4),
        pltpu.make_async_copy(inv_hi_in, inv_hi, local_sem.at[5]),
        pltpu.make_async_copy(inv_lo_in, inv_lo, local_sem.at[6]),
        pltpu.make_async_copy(weight, wts.at[slot], local_sem.at[7]),
        pltpu.make_async_copy(filt_in, filt, local_sem.at[10]),
    ]
    for load in loads:
        load.start()

    barrier = pltpu.get_barrier_semaphore()

    def greet(to):
        pl.semaphore_signal(barrier, inc=1, device_id=to, device_id_type=MESH)

    def near(k):
        other = lax.rem(x * 2 + core + k, NEAR)
        return other // 2, lax.rem(other, 2)

    def greet_near(k, carry):
        x_, core_ = near(k)
        greet(device(x_=x_, core_=core_))
        return carry

    lax.fori_loop(1, NEAR, greet_near, 0)
    for k in range(1, PEERS):
        greet(device(zl_=ring(k, zl)))
        greet(device(y_=ring(k, y)))
    after, before = lax.rem(ctx + 1, 16), lax.rem(ctx + 15, 16)
    greet((after, fsdp))
    greet((before, fsdp))
    greet(device(zl_=3 - zl, zh_=1 - zh))
    greet(device(zl_=ring(2, zl), zh_=1 - zh))

    own_taps = jnp.concatenate([taps_in[...].astype(F32), jnp.zeros((8 - TAPS, TAPCOLS), F32)], axis=0)
    own_taps = jnp.concatenate([own_taps[:, : TAPCOLS // 2], own_taps[:, TAPCOLS // 2 :]], axis=0)
    taps_all[here, zh] = own_taps.astype(BF16)

    tail_load.wait()

    def pack(part, group):
        rows = tail[:, part * CHANNELS + group * GROUP : part * CHANNELS + (group + 1) * GROUP].astype(F32)[16 - HALO :]
        packed = jnp.concatenate([rows[:, :HALF], rows[:, HALF:]], axis=0)
        return packed.astype(BF16)

    for group in range(GROUPS):
        halo_out[group, 0] = pack(1, group)
        halo_out[group, 1] = pack(2, group)
        halo_out[GROUPS + group // 2, group % 2] = pack(0, group)

    pl.semaphore_wait(barrier, NEAR - 1 + 2 * (PEERS - 1) + 4)

    def far_taps(j, to_zl):
        ref = taps_all.at[here, zh]
        return remote(ref, ref, wt_send.at[j], wt_recv, device(zl_=to_zl, zh_=1 - zh))

    @pl.when(zl == 0)
    def _():
        far_taps(1, 2).start()
        far_taps(0, 3).start()

    @pl.when(zl == 3)
    def _():
        far_taps(1, 1).start()
        far_taps(0, 0).start()

    def tap_copy(k):
        x_, core_ = near(k)
        return remote(taps_all.at[here], taps_all.at[here], tap_send.at[k], tap_recv.at[here], device(x_=x_, core_=core_))

    def tap_arrival(k):
        x_, core_ = near(k)
        there = x_ * 2 + core_
        return remote(taps_all.at[there], taps_all.at[there], tap_send.at[k], tap_recv.at[there], device(x_=x_, core_=core_))

    def halo_copy(at):
        return remote(halo_out.at[at], halo_in.at[at], halo_send.at[at], halo_recv.at[at], (after, fsdp))

    for group in range(GROUPS):
        halo_copy(group).start()

    ref = taps_all.at[here, 1 - zh]
    remote(ref, ref, wt_send.at[0], wt_recv, device(zl_=3 - zl, zh_=1 - zh)).wait_recv()
    for k in (4, 3, 5, 2, 6, 1, 7):
        tap_copy(k).start()

    def quarter(ref, which):
        return ref.at[pl.ds(pl.multiple_of(which * GROUP, GROUP), GROUP)]

    mate = device(core_=1 - core)
    mate_copy = remote(weight, wts.at[slot], wm_sem.at[0], wm_sem.at[1], mate)

    def far_copy(j, to_zl):
        return remote(quarter(weight, y), quarter(wts.at[slot], y), wz_send.at[j], wz_recv, device(zl_=to_zl, zh_=1 - zh))

    @pl.when(zl == 0)
    def _():
        far_copy(1, 2).start()
        far_copy(0, 3).start()

    @pl.when(zl == 3)
    def _():
        far_copy(1, 1).start()
        far_copy(0, 0).start()

    loads[2].wait()
    loads[3].wait()
    loads[8].wait()
    mine_filt = filt[:, pl.ds(pl.multiple_of(lax.rem(zl, FILTERS // WIDTH) * WIDTH, WIDTH), WIDTH)]
    for part in range(4):
        rows = pl.ds(part * 256, 256)
        spec[rows, :] = dot(fwd_hi[rows, :], mine_filt) + dot(fwd_lo[rows, :], mine_filt)

    @pl.when(y == 0)
    def _():
        prev[...] = jnp.zeros(prev.shape, BF16)

    loads[0].wait()
    loads[1].wait()
    loads[4].wait()

    for k in range(1, NEAR):
        tap_arrival(k).wait_recv()
    for shard in range(SHARDS):
        block = taps_all[shard // 4 * 2 + shard % 2, shard // 2 % 2].astype(F32)
        taps[:, pl.ds(shard * TAPCOLS, TAPCOLS // 2)] = block[:8]
        taps[:, pl.ds(shard * TAPCOLS + TAPCOLS // 2, TAPCOLS // 2)] = block[8:]

    keep = jnp.where(ctx > 0, 1.0, 0.0).astype(F32)

    def unpack(at, which, begin):
        block = halo_in[at, which].astype(F32) * keep
        halo[:, pl.ds(pl.multiple_of(begin, HALF), HALF)] = block[:HALO]
        halo[:, pl.ds(pl.multiple_of(begin + HALF, HALF), HALF)] = block[HALO:]

    def short_filter(begin):
        columns = pl.ds(pl.multiple_of(begin, 128), 128)
        rows = jnp.concatenate([halo[:, columns], ext[:, columns].astype(F32)], axis=0)
        weights = taps[:, columns]
        total = weights[0:1] * rows[HALO:]
        for lag in range(1, TAPS):
            total = total + weights[lag : lag + 1] * pltpu.roll(rows, lag, 0)[HALO:]
        return total

    def own_rows(which):
        return pl.ds(pl.multiple_of(which * ROWS, ROWS), ROWS)

    def across_first(k):
        return (lax.rem(zl + 2, PEERS), 3 - zl, zl + 1 - 2 * lax.rem(zl, 2))[k - 1]

    def zf_copy(i, k):
        q = across_first(k)
        return remote(prod.at[i, q], cur.at[i, own_rows(zl)], zf_send.at[i, k], zf_recv.at[i, zl], device(zl_=q))

    def zf_arrival(i, k):
        q = across_first(k)
        return remote(prod.at[i, q], cur.at[i, own_rows(q)], zf_send.at[i, k], zf_recv.at[i, q], device(zl_=q))

    def products(i):
        group = i // 2

        @pl.when(lax.rem(i, 2) == 0)
        def _():
            halo_copy(group).wait_recv()
            unpack(group, 0, CHANNELS + group * GROUP)
            unpack(group, 1, 2 * CHANNELS + group * GROUP)

        def one(q):
            begin = i * CHUNK + q * WIDTH
            keys = short_filter(CHANNELS + begin)
            values = short_filter(2 * CHANNELS + begin)
            return (keys * values).astype(BF16)

        for k in range(1, PEERS):
            prod[i, across_first(k)] = one(across_first(k))
            zf_copy(i, k).start()
        cur[i, own_rows(zl), :] = one(zl)

        @pl.when(i == 1)
        def _():
            for at in (GROUPS, GROUPS + 1):
                halo_copy(at).start()


    def yf_copy(i):
        return remote(cur.at[i], prev.at[i], yf_sem.at[0, i], yf_sem.at[1, i], device(y_=ring(1, y)))

    def onward(i):
        for k in range(1, PEERS):
            zf_arrival(i, k).wait_recv()

        @pl.when(y < PEERS - 1)
        def _():
            yf_copy(i).start()

    def zb_copy(i, k):
        q = across_first(k)
        return remote(convs.at[i, own_rows(q)], back.at[i, zl], zb_send.at[i, k], zb_recv.at[i, zl], device(zl_=q))

    def zb_arrival(i, k):
        q = across_first(k)
        return remote(convs.at[i, own_rows(q)], back.at[i, q], zb_send.at[i, k], zb_recv.at[i, q], device(zl_=q))

    def convolve(i):
        @pl.when(y > 0)
        def _():
            yf_copy(i).wait_recv()

        def frequencies(part, carry):
            real = pl.ds(pl.multiple_of(part * 128, 128), 128)
            imag = pl.ds(pl.multiple_of(SPAN + part * 128, 128), 128)
            both = jnp.concatenate([cur[i], prev[i]], axis=1)
            re = dot(fwd_hi[real, :], both) + dot(fwd_lo[real, :], both)
            im = dot(fwd_hi[imag, :], both) + dot(fwd_lo[imag, :], both)
            sign = jnp.where(part < 2, 1.0, -1.0).astype(F32)
            a = re[:, :WIDTH] - sign * im[:, WIDTH:]
            b = im[:, :WIDTH] + sign * re[:, WIDTH:]
            hr, hi = spec[real, :], spec[imag, :]
            yr = hr * a - hi * b
            yi = hr * b + hi * a
            yr_hi, yi_hi = yr.astype(BF16), yi.astype(BF16)
            y_hi[real, :] = yr_hi
            y_hi[imag, :] = yi_hi
            y_lo[real, :] = (yr - yr_hi.astype(F32)).astype(BF16)
            y_lo[imag, :] = (yi - yi_hi.astype(F32)).astype(BF16)
            return carry

        lax.fori_loop(0, 4, frequencies, 0)

        def positions(part):
            rows = own_rows(part)
            both = dot(inv_hi[rows, :], jnp.concatenate([y_hi[...], y_lo[...]], axis=1))
            got = both[:, :WIDTH] + both[:, WIDTH:] + dot(inv_lo[rows, :], y_hi[...])
            return got.astype(BF16)

        for k in range(1, PEERS):
            convs[i, own_rows(across_first(k)), :] = positions(across_first(k))
            zb_copy(i, k).start()
        back[i, zl] = positions(zl)

    left, right = ring(3, x), ring(1, x)

    def half(i, source, at):
        return gated.at[i, source, pl.ds(at * (ROWS // 2), ROWS // 2)]

    def xg_copy(i, to, at, which):
        ref = half(i, x, which)
        return remote(ref, ref, xg_send.at[i, at, which], xg_recv.at[i, at, which], device(x_=to))

    def xg_arrival(i, source, at, which):
        ref = half(i, source, which)
        return remote(ref, ref, xg_send.at[i, at, which], xg_recv.at[i, at, which], device(x_=source))

    def xr_copy(i, source, to, at):
        ref = half(i, source, at)
        return remote(ref, ref, xr_send.at[i, at], xr_recv.at[i, at], device(x_=to))

    def gate(i):
        @pl.when(i == 0)
        def _():
            for at in (GROUPS, GROUPS + 1):
                halo_copy(at).wait_recv()
            for group in range(GROUPS):
                unpack(GROUPS + group // 2, group % 2, group * GROUP)

        for k in range(1, PEERS):
            zb_arrival(i, k).wait_recv()
        for q in range(PEERS):
            query = short_filter(i * CHUNK + q * WIDTH)
            gated[i, x, :, q * WIDTH : (q + 1) * WIDTH] = (query * back[i, q].astype(F32)).astype(BF16)
        xg_copy(i, right, 0, 0).start()
        xg_copy(i, left, 1, 1).start()
        xg_copy(i, right, 0, 1).start()
        xg_copy(i, left, 1, 0).start()

    def relay(i):
        xg_arrival(i, left, 0, 0).wait_recv()
        xr_copy(i, left, right, 0).start()
        xg_arrival(i, right, 1, 1).wait_recv()
        xr_copy(i, right, left, 1).start()

    def far_arrivals(i):
        across = ring(2, x)
        xg_arrival(i, left, 0, 1).wait_recv()
        xg_arrival(i, right, 1, 0).wait_recv()
        xr_copy(i, across, left, 0).wait_recv()
        xr_copy(i, across, right, 1).wait_recv()

    def project(group, zh_):
        lhs = [gated[2 * group + part].reshape(PEERS * ROWS, CHUNK) for part in range(2)]

        def block(c, carry):
            j = zh_ * 2 + c
            term = acc[j]
            for part in range(2):
                term = term + dot(lhs[part], wts[j, pl.ds(pl.multiple_of(group * GROUP + part * CHUNK, CHUNK), CHUNK), :])
            acc[j] = term
            return carry

        lax.fori_loop(0, 2, block, 0)

    def wy_copy(k):
        ref = quarter(wts.at[far_slot], ring(k, y))
        return remote(ref, ref, wy_send.at[k], wy_recv.at[k], device(y_=ring(3, y)))

    def wy_arrival(k):
        ref = quarter(wts.at[far_slot], ring(k + 1, y))
        return remote(ref, ref, wy_send.at[k], wy_recv.at[k], device(y_=ring(1, y)))

    def wc_copy(which):
        ref = quarter(wts.at[far_slot], which)
        return remote(ref, ref, wc_send.at[which], wc_recv.at[which], mate)

    def wc_arrival(which):
        ref = quarter(wts.at[(1 - zh) * 2 + 1 - core], which)
        return remote(ref, ref, wc_send.at[which], wc_recv.at[which], mate)

    def columns_first():
        far = quarter(wts.at[far_slot], y)
        remote(far, far, wz_send.at[0], wz_recv, device(zl_=3 - zl, zh_=1 - zh)).wait_recv()
        wy_copy(0).start()
        wc_copy(y).start()

    def columns_next(k):
        wy_arrival(k - 1).wait_recv()

        @pl.when(k < PEERS - 1)
        def _():
            wy_copy(k).start()

        wc_copy(ring(k, y)).start()

    loads[5].wait()
    loads[6].wait()
    acc[...] = jnp.zeros(acc.shape, F32)

    def step(t, carry):
        @pl.when(t < CHUNKS)
        def _():
            products(t)

        @pl.when(jnp.logical_and(t >= 2, t < CHUNKS + 2))
        def _():
            onward(t - 2)

        @pl.when(jnp.logical_and(t >= 3, t < CHUNKS + 3))
        def _():
            convolve(t - 3)

        @pl.when(jnp.logical_and(t >= 4, t < CHUNKS + 4))
        def _():
            gate(t - 4)

        @pl.when(t >= 5)
        def _():
            relay(t - 5)

        @pl.when(t == 6)
        def _():
            mate_copy.start()

        @pl.when(t == 4)
        def _():
            columns_first()

        @pl.when(jnp.logical_or(t == 6, jnp.logical_or(t == 8, t == 10)))
        def _():
            columns_next((t - 4) // 2)

        @pl.when(t == 9)
        def _():
            loads[7].wait()
            mate_copy.wait_recv()

        @pl.when(t >= 9)
        def _():
            far_arrivals(2 * (t - 9))
            far_arrivals(2 * (t - 9) + 1)
            project(t - 9, zh)

        return carry

    lax.fori_loop(0, CHUNKS + 4, step, 0)

    def out_columns(x_, zh_):
        return out.at[:, pl.ds(pl.multiple_of(x_ * OUT + zh_ * (OUT // 2), OUT // 2), OUT // 2)]

    def out_copy(zh_, k):
        q = ring(k, x)
        return remote(outs.at[zh_, q], out_columns(x, zh_), o_send.at[zh_, k], o_recv.at[zh_, x], device(x_=q))

    def out_arrival(zh_, k):
        q = ring(k, x)
        return remote(outs.at[zh_, q], out_columns(q, zh_), o_send.at[zh_, k], o_recv.at[zh_, q], device(x_=q))

    def out_own(zh_):
        return pltpu.make_async_copy(outs.at[zh_, x], out_columns(x, zh_), own_sem.at[zh_])

    last = GROUPS - 1

    def finish(zh_):
        def one(k):
            q = ring(k, x)
            lhs = jnp.concatenate([gated[2 * last, q], gated[2 * last + 1, q]], axis=1)
            for c in range(2):
                j = zh_ * 2 + c
                total = acc[j, own_rows(q), :] + dot(lhs, wts[j, last * GROUP :, :])
                outs[zh_, q, :, c * COLS : (c + 1) * COLS] = total.astype(BF16)

        def send(step, carry):
            k = lax.rem(step, PEERS - 1) + 1
            one(k)
            out_copy(zh_, k).start()
            return carry

        lax.fori_loop(1, PEERS, send, 0)
        one(0)
        out_own(zh_).start()

    relay(CHUNKS - 1)

    def arrived(which, carry):
        wc_arrival(which).wait_recv()
        return carry

    lax.fori_loop(0, PEERS, arrived, 0)

    def project_far(group, carry):
        project(group, 1 - zh)
        return carry

    lax.fori_loop(0, last, project_far, 0)
    for i in range(2 * last, CHUNKS):
        far_arrivals(i)
    finish(zh)
    finish(1 - zh)
    for zh_ in range(2):
        out_own(zh_).wait()
        for k in range(1, PEERS):
            out_arrival(zh_, k).wait_recv()

    mate_copy.wait_send()
    for at in range(GROUPS + 2):
        halo_copy(at).wait_send()

    for k in range(1, NEAR):
        tap_copy(k).wait_send()

    @pl.when(jnp.logical_or(zl == 0, zl == 3))
    def _():
        far_copy(0, 3 - zl).wait_send()
        far_copy(1, ring(2, zl)).wait_send()
        far_taps(0, 3 - zl).wait_send()
        far_taps(1, ring(2, zl)).wait_send()

    for k in range(1, PEERS):
        wy_copy(k - 1).wait_send()
        out_copy(0, k).wait_send()
        out_copy(1, k).wait_send()
    for which in range(PEERS):
        wc_copy(which).wait_send()

    def sent_chunk(i, carry):
        for k in range(1, PEERS):
            zf_copy(i, k).wait_send()
            zb_copy(i, k).wait_send()
        for which in range(2):
            xg_copy(i, right, 0, which).wait_send()
            xg_copy(i, left, 1, which).wait_send()
        xr_copy(i, left, right, 0).wait_send()
        xr_copy(i, right, left, 1).wait_send()

        @pl.when(y < PEERS - 1)
        def _():
            yf_copy(i).wait_send()

        return carry

    lax.fori_loop(0, CHUNKS, sent_chunk, 0)


def shards(features, short_weight, long_filter, out_weight):
    matrices = [jnp.asarray(m) for m in transform_matrices()]
    anywhere = pl.BlockSpec(memory_space=pl.ANY)
    dma = pltpu.SemaphoreType.DMA
    result = pl.pallas_call(
        mixer_kernel,
        name="mixer",
        out_shape=jax.ShapeDtypeStruct((ROWS, CHANNELS), BF16),
        in_specs=[anywhere, pl.BlockSpec(memory_space=pltpu.VMEM)] + [anywhere] * 6,
        out_specs=anywhere,
        scratch_shapes=[
            pltpu.VMEM((ROWS, 3 * CHANNELS), BF16),
            pltpu.VMEM((16, 3 * CHANNELS), BF16),
            pltpu.VMEM((SPAN, FILTERS), BF16),
            pltpu.VMEM((GROUPS + 2, 2, 2 * HALO, HALF), BF16),
            pltpu.VMEM((GROUPS + 2, 2, 2 * HALO, HALF), BF16),
            pltpu.VMEM((HALO, 3 * CHANNELS), F32),
            pltpu.VMEM((NEAR, 2, 16, TAPCOLS // 2), BF16),
            pltpu.VMEM((8, 3 * CHANNELS), F32),
            pltpu.VMEM((2 * SPAN, SPAN), BF16),
            pltpu.VMEM((2 * SPAN, SPAN), BF16),
            pltpu.VMEM((SPAN, 2 * SPAN), BF16),
            pltpu.VMEM((SPAN, 2 * SPAN), BF16),
            pltpu.VMEM((2 * SPAN, WIDTH), F32),
            pltpu.VMEM((2 * SPAN, WIDTH), BF16),
            pltpu.VMEM((2 * SPAN, WIDTH), BF16),
            pltpu.VMEM((CHUNKS, PEERS, ROWS, WIDTH), BF16),
            pltpu.VMEM((CHUNKS, SPAN, WIDTH), BF16),
            pltpu.VMEM((CHUNKS, SPAN, WIDTH), BF16),
            pltpu.VMEM((CHUNKS, SPAN, WIDTH), BF16),
            pltpu.VMEM((CHUNKS, PEERS, ROWS, WIDTH), BF16),
            pltpu.VMEM((CHUNKS, PEERS, ROWS, CHUNK), BF16),
            pltpu.VMEM((PEERS, CHANNELS, COLS), BF16),
            pltpu.VMEM((PEERS, PEERS * ROWS, COLS), F32),
            pltpu.VMEM((2, PEERS, ROWS, OUT // 2), BF16),
            dma((11,)), dma((GROUPS + 2,)), dma((GROUPS + 2,)), dma((2,)), dma, dma((NEAR,)), dma((NEAR,)),
            dma((CHUNKS, PEERS)), dma((CHUNKS, PEERS)), dma((2, CHUNKS)), dma((CHUNKS, PEERS)), dma((CHUNKS, PEERS)),
            dma((CHUNKS, 2, 2)), dma((CHUNKS, 2, 2)), dma((CHUNKS, 2)), dma((CHUNKS, 2)),
            dma((2,)), dma, dma((PEERS,)), dma((PEERS,)), dma((2,)), dma((PEERS,)), dma((PEERS,)), dma((2, PEERS)), dma((2, PEERS)), dma((2,)),
        ],
        compiler_params=pltpu.CompilerParams(collective_id=0, has_side_effects=True, vmem_limit_bytes=56 * 2**20),
    )(features[0], short_weight, long_filter, out_weight, *matrices)
    return result[None]


def solution(mesh):
    placed = (P("fsdp", "ctx", None), P(None, "fsdp"), P(), P(None, "fsdp"))
    return jax.shard_map(
        shards, mesh=mesh, in_specs=placed, out_specs=P("fsdp", "ctx", None), check_vma=False
    )
```
